256 devices in a mesh: group: 32 (over y, x, core), tensor: 8 (over z).
Axes of the slice: x: 4, y: 4, z: 8, core: 2. Of those that a mesh axis runs over, the one named last changes fastest.
Arguments:
- owner: int32 [1024, 1], P('group'), may hold values from 0 to 31; in each aligned block of 32 rows (0 to 31, 32 to 63, ...) at most 2 rows name the same one
- cont_q: bfloat16 [1024, 8, 8192], P('group', None, 'tensor'), may hold values from -360 to 360
- continuation_keys: bfloat16 [1024, 8, 1024], P('group', None, 'tensor'), may hold values from -6 to 6
- continuation_values: bfloat16 [1024, 8, 1024], P('group', None, 'tensor'), may hold values from -6 to 6
- cached_prompt_keys: bfloat16 [32, 4096, 1024], P('group', None, 'tensor'), may hold values from -6 to 6
- cached_prompt_values: bfloat16 [32, 4096, 1024], P('group', None, 'tensor'), may hold values from -6 to 6
- out_weight: bfloat16 [8192, 8192], P('tensor', 'group'), may hold values from -0.0625 to 0.0625
Outputs:
- projected: bfloat16 [8192, 8192], P('group', 'tensor')
The draws below stay inside these ranges and needn't reach their ends.
Inputs may be any that keep to these rules, and one draw needn't show every extreme that they name: `owner`: among the 32 continuations of each group (rows g * 32 to (g + 1) * 32 - 1) no prompt is named more than 2 times, a bound that some block reaches. Every prompt has a continuation somewhere; a continuation may sit on its own prompt's group.
All inputs are finite; a program needn't handle non-finite values.
Results may differ from the reference program's by a relative error of at most 0.0057.
Values may be sent and summed in bfloat16 or wider, within the bound.
No kernel may reach another device: no remote copies, remote signals or barrier semaphores. Data moves between devices by JAX's collectives and lax.ppermute only.
A program may use at most 128 MiB of HBM per device.

```python
import math
import jax
import jax.numpy as jnp
import numpy as np
from jax import lax

D = 8192
HQ = 64
KEY_VALUE_HEADS = 8
HEAD_DIMENSION = 128
PROMPT_LENGTH = 4096
CONTINUATION_LEN = 8
HOST = 32
SLOT = 2
CONTINUATION_NUM = 1024
N_GROUP = 32


def draw_cont_q(key, part):
    key = jax.random.fold_in(key, 7)
    shape = (CONTINUATION_NUM, CONTINUATION_LEN, HQ * HEAD_DIMENSION)
    base = jax.random.truncated_normal(key, -6.0, 6.0, shape, jnp.float32)
    return base.astype(jnp.bfloat16)


def steps_of(own_key, extent, shards, least, largest):
    gain = 1.0
    for dim, blocks in shards:
        heights = jax.random.uniform(jax.random.fold_in(jax.random.fold_in(own_key, 6), dim), (blocks,), jnp.float32, least / len(shards), largest / len(shards))
        gain = gain * jnp.repeat(jnp.exp(heights), extent[dim] // blocks).reshape((-1,) + (1,) * (len(extent) - 1 - dim))
    return gain


def shared_out(own_key, own, number, rows, count, top, limit, lean):
    sequence = jax.random.permutation(own_key, count)
    crowded, usual = shares(count, rows * top, limit, lean, True), shares(count, rows * top, limit, lean, False)
    places = jnp.arange(count)

    def named(sizes, offset_by):
        used = int((sizes > 0).sum())
        fixed = max(1, used // 4)
        moved = fixed + (places - fixed + offset_by * (used - fixed)) % max(1, count - fixed)
        return jnp.zeros((count,), jnp.int32).at[sequence[jnp.where(places < fixed, places, moved)]].set(jnp.asarray(sizes, jnp.int32))

    sizes = jnp.where(number % 4 == 0, named(crowded, number // 4), named(usual, number - number // 4 - 1))
    mixed = jax.random.permutation(jax.random.fold_in(own, 3), count)
    source_of, receiver = mixed[0:count // 2 * 2:2], mixed[1:count // 2 * 2:2]
    slack = jnp.minimum(sizes[source_of] - 1, limit - sizes[receiver]) // 2
    slack = jnp.where((source_of == sequence[0]) | (receiver == sequence[0]) | (sizes[receiver] == 0), 0, jnp.maximum(slack, 0))
    moved = jax.random.randint(jax.random.fold_in(own, 4), (count // 2,), 0, 1 << 20) % (slack + 1)
    sizes = sizes.at[source_of].add(-moved).at[receiver].add(moved)
    labels = jnp.searchsorted(jnp.cumsum(sizes), jnp.arange(rows * top), side="right").astype(jnp.int32)
    table = labels.reshape(top, rows).T
    table = table[jax.random.permutation(jax.random.fold_in(own, 1), rows)]
    offset_by = jax.random.randint(jax.random.fold_in(own, 2), (rows, 1), 0, top)
    return jnp.take_along_axis(table, (jnp.arange(top)[None, :] + offset_by) % top, axis=1)


def shares(count, total, bound, slope, full):
    weights = [(1 << 20) // math.isqrt(grade ** slope) + 1 for grade in range(1, count + 1)]
    largest = bound if full else min(bound, max(-(-total // count), total * weights[0] // sum(weights)))
    least = 1 if total - largest >= count - 1 else 0
    counts, rest = [largest] + [least] * (count - 1), total - largest - least * (count - 1)
    while rest > 0:
        movable = [i for i in range(1, count) if counts[i] < largest] or [i for i in range(1, count) if counts[i] < bound]
        pool, budget = sum([weights[i] for i in movable]), rest
        for i in movable:
            extra = min(bound - counts[i], max(1, budget * weights[i] // pool), rest)
            counts[i] = counts[i] + extra
            rest = rest - extra
    return np.array(counts)


def centred(stream_key, shape, scale, bound, cuts=(), dtype=jnp.bfloat16):
    factor_of = steps_of(stream_key, shape, cuts, -0.22, 0.18) if cuts else 1.0
    result = jax.random.normal(stream_key, shape, jnp.float32) * scale * factor_of
    return jnp.minimum(jnp.maximum(result, -bound), bound).astype(dtype)


def setup_inputs(seed: int = 0) -> dict:
    arg_keys = jax.random.split(jax.random.key(seed), 8)
    owner_keys = jax.random.split(jax.random.fold_in(arg_keys[0], 1), CONTINUATION_NUM // HOST)
    owner_turns = jax.random.permutation(jax.random.fold_in(arg_keys[0], 3), CONTINUATION_NUM // HOST)
    owner = jax.vmap(lambda own, number: shared_out(jax.random.fold_in(arg_keys[0], 2), own, number, HOST, N_GROUP, 1, SLOT, 2))(owner_keys, owner_turns).reshape((CONTINUATION_NUM, 1))
    cont_q = draw_cont_q(jax.random.fold_in(arg_keys[7], 71), 0)
    continuation_keys = centred(arg_keys[2], (CONTINUATION_NUM, CONTINUATION_LEN, KEY_VALUE_HEADS * HEAD_DIMENSION), 1.0, 6.0, ((0, 32), (2, 8)))
    continuation_values = centred(arg_keys[3], (CONTINUATION_NUM, CONTINUATION_LEN, KEY_VALUE_HEADS * HEAD_DIMENSION), 1.0, 6.0, ((0, 32), (2, 8)))
    cached_prompt_keys = centred(arg_keys[4], (N_GROUP, PROMPT_LENGTH, KEY_VALUE_HEADS * HEAD_DIMENSION), 1.0, 6.0, ((0, 32), (2, 8)))
    cached_prompt_values = centred(arg_keys[5], (N_GROUP, PROMPT_LENGTH, KEY_VALUE_HEADS * HEAD_DIMENSION), 1.0, 6.0, ((0, 32), (2, 8)))
    out_weight = centred(arg_keys[6], (HQ * HEAD_DIMENSION, D), (HQ * HEAD_DIMENSION) ** -0.5, 0.0625, ((0, 8), (1, 32)))
    return dict(owner=owner, cont_q=cont_q, continuation_keys=continuation_keys, continuation_values=continuation_values, cached_prompt_keys=cached_prompt_keys, cached_prompt_values=cached_prompt_values, out_weight=out_weight)


def prefix_partial(query, keys, values):
    count, steps, width = query.shape
    heads = keys.shape[1] // HEAD_DIMENSION
    block = math.gcd(count, 8)
    key_heads = keys.reshape(keys.shape[0], heads, HEAD_DIMENSION)
    value_heads = values.reshape(values.shape[0], heads, HEAD_DIMENSION)

    def one_block(rows):
        split = rows.reshape(block, steps, heads, -1, HEAD_DIMENSION)
        scores = jnp.einsum("bcjgd,ljd->bcjgl", split, key_heads, preferred_element_type=jnp.float32) * (HEAD_DIMENSION ** -0.5)
        top = jnp.max(scores, axis=-1)
        expd = jnp.exp(scores - top[..., None])
        total = jnp.sum(expd, axis=-1)
        summed = jnp.einsum("bcjgl,ljd->bcjgd", expd.astype(jnp.bfloat16), value_heads, preferred_element_type=jnp.float32)
        return summed / total[..., None], top, total

    outs, tops, totals = lax.map(one_block, query.reshape(count // block, block, steps, width))
    return (outs.reshape(count, steps, -1, HEAD_DIMENSION), tops.reshape(count, steps, -1), totals.reshape(count, steps, -1))


def own_partial(query, keys, values):
    count, steps, width = query.shape
    heads = keys.shape[2] // HEAD_DIMENSION
    split = query.reshape(count, steps, heads, -1, HEAD_DIMENSION)
    key_heads = keys.reshape(count, steps, heads, HEAD_DIMENSION)
    value_heads = values.reshape(count, steps, heads, HEAD_DIMENSION)
    scores = jnp.einsum("bcjgd,bejd->bcjge", split, key_heads, preferred_element_type=jnp.float32) * (HEAD_DIMENSION ** -0.5)
    allowed = jnp.arange(steps)[None, :] <= jnp.arange(steps)[:, None]
    scores = jnp.where(allowed[None, :, None, None, :], scores, -1e30)
    top = jnp.max(scores, axis=-1)
    expd = jnp.exp(scores - top[..., None])
    total = jnp.sum(expd, axis=-1)
    summed = jnp.einsum("bcjge,bejd->bcjgd", expd.astype(jnp.bfloat16), value_heads, preferred_element_type=jnp.float32)
    return (summed / total[..., None]).reshape(count, steps, -1, HEAD_DIMENSION), top.reshape(count, steps, -1), total.reshape(count, steps, -1)


def combine(first, second):
    out_a, top_a, tot_a = first
    out_b, top_b, tot_b = second
    peak = jnp.maximum(top_a, top_b)
    weight_a = jnp.exp(top_a - peak) * tot_a
    weight_b = jnp.exp(top_b - peak) * tot_b
    mixed = (weight_a[..., None] * out_a + weight_b[..., None] * out_b) / (weight_a + weight_b)[..., None]
    return mixed.reshape(mixed.shape[0], mixed.shape[1], -1).astype(jnp.bfloat16)


def reference(owner, cont_q, continuation_keys, continuation_values, cached_prompt_keys, cached_prompt_values, out_weight):
    def one(items):
        prompt, query, keys, values = items
        ckeys = lax.dynamic_index_in_dim(cached_prompt_keys, prompt, 0, keepdims=False)
        cvalues = lax.dynamic_index_in_dim(cached_prompt_values, prompt, 0, keepdims=False)
        first = prefix_partial(query[None], ckeys, cvalues)
        second = own_partial(query[None], keys[None], values[None])
        return combine(first, second)[0]

    attn = lax.map(one, (owner[:, 0].astype(jnp.int32), cont_q, continuation_keys, continuation_values))
    flat = attn.reshape(-1, attn.shape[-1])
    return jnp.dot(flat, out_weight, preferred_element_type=jnp.float32).astype(jnp.bfloat16)
```

```python
import functools

import jax
import jax.numpy as jnp
from jax import lax
from jax.experimental import pallas as pl
from jax.experimental.pallas import tpu as pltpu
from jax.sharding import Mesh, PartitionSpec as P

HEAD = 128
GROUPS = 32
SLOT = 2
HOST = 32
STEPS = 8
HEADS = 8
PROMPT = 4096
RING = 8
GROUP = ("y", "x", "c")
PARTS = (4, 4)
SCALE2 = HEAD**-0.5 * 1.4426950408889634


def smem():
    return pl.BlockSpec(memory_space=pltpu.SMEM)


def vmem():
    return pl.BlockSpec(memory_space=pltpu.VMEM)


def hbm():
    return pl.BlockSpec(memory_space=pl.ANY)


def each_place(owner_ref, used_ref, act):
    for g in range(GROUPS):
        used_ref[g] = 0

    @pl.loop(0, HOST)
    def _(c):
        prompt = owner_ref[c, 0]
        rank = used_ref[prompt]
        used_ref[prompt] = rank + 1
        act(c, prompt * SLOT + rank)


def pack_kernel(owner_ref, q_ref, k_ref, v_ref, *rest):
    outs, used_ref = rest[:-1], rest[-1]
    for out in outs:
        out[...] = jnp.zeros_like(out)

    def act(c, place):
        first = 0
        for part, heads in enumerate(PARTS):
            width = heads * HEAD
            outs[part][place, :, 0:width] = q_ref[c, :, first : first + width]
            first += width
        width = PARTS[0] * HEAD
        outs[0][place, :, width : width + HEAD] = k_ref[c]
        outs[0][place, :, width + HEAD : width + 2 * HEAD] = v_ref[c]

    each_place(owner_ref, used_ref, act)


def pack(owner, q, k, v):
    widths = [heads * HEAD for heads in PARTS]
    widths[0] += 2 * HEAD
    return pl.pallas_call(
        pack_kernel,
        out_shape=[
            jax.ShapeDtypeStruct((GROUPS * SLOT, STEPS, width), jnp.bfloat16) for width in widths
        ],
        in_specs=[smem(), vmem(), vmem(), vmem()],
        out_specs=[vmem()] * len(PARTS),
        scratch_shapes=[pltpu.SMEM((GROUPS,), jnp.int32)],
        compiler_params=pltpu.CompilerParams(vmem_limit_bytes=16 * 2**20),
        name="pack",
    )(owner, q, k, v)


def unpack_kernel(owner_ref, got_ref, out_ref, used_ref):
    def act(c, place):
        out_ref[c] = got_ref[place]

    each_place(owner_ref, used_ref, act)


def unpack(owner, got):
    return pl.pallas_call(
        unpack_kernel,
        out_shape=jax.ShapeDtypeStruct((HOST,) + got.shape[1:], got.dtype),
        in_specs=[smem(), vmem()],
        out_specs=vmem(),
        scratch_shapes=[pltpu.SMEM((GROUPS,), jnp.int32)],
        compiler_params=pltpu.CompilerParams(vmem_limit_bytes=16 * 2**20),
        name="unpack",
    )(owner, got)


def prompt_kernel(k_ref, v_ref, after_ref, kt_ref, ve_ref):
    for first in range(0, PROMPT, 512):
        rows = slice(first, first + 512)
        kt_ref[:, rows] = k_ref[0, rows, :].astype(jnp.float32).T.astype(jnp.bfloat16)
        ve_ref[rows, 0:HEAD] = v_ref[0, rows, :]
        lane = lax.broadcasted_iota(jnp.int32, (512, HEAD), 1)
        ve_ref[rows, HEAD:] = jnp.where(lane == 0, 1.0, 0.0).astype(jnp.bfloat16)


def prompt_ready(keys, values, after):
    return pl.pallas_call(
        prompt_kernel,
        out_shape=[
            jax.ShapeDtypeStruct((HEAD, PROMPT), jnp.bfloat16),
            jax.ShapeDtypeStruct((PROMPT, 2 * HEAD), jnp.bfloat16),
        ],
        in_specs=[vmem(), vmem(), hbm()],
        out_specs=[vmem(), vmem()],
        compiler_params=pltpu.CompilerParams(vmem_limit_bytes=16 * 2**20),
        cost_estimate=pl.CostEstimate(flops=0, bytes_accessed=8 * 2**20, transcendentals=0),
        name="prompt_ready",
    )(keys, values, after)


TILE = 8
ROWS = 256


def attend_kernel(heads, start, tiles, block_cols, q_ref, own_ref, kt_ref, ve_ref, *refs):
    out_ref, scratch = refs[-7], refs[-6:]
    if start:
        out_ref[0 : start * TILE] = refs[0][...]
    each = TILE * STEPS
    base = PARTS[0] * HEAD
    s_refs, p_refs, peaks = scratch[0:2], scratch[2:4], scratch[4:6]

    def flat(ref, tile, first):
        block = ref[pl.ds((start + tile) * TILE, TILE), :, first : first + HEAD].astype(jnp.float32)
        return block.reshape(each, HEAD)

    def weights(scores, peak):
        return jnp.exp2((scores - peak) * SCALE2).astype(jnp.bfloat16)

    def stages(tile, slot, do):
        s_ref, peak_ref = s_refs[slot], peaks[slot]
        old_s, old_peak, new_p, old_p = s_refs[1 - slot], peaks[1 - slot], p_refs[1 - slot], p_refs[slot]
        top = None
        if do[0]:
            query = jnp.concatenate(
                [flat(q_ref, tile, h * HEAD) for h in range(heads)], axis=0
            ).astype(jnp.bfloat16)
            own_k = flat(own_ref, tile, base)
            own_k = jnp.concatenate([own_k, jnp.zeros_like(own_k)], axis=0).astype(jnp.bfloat16)
            own = lax.dot_general(
                query, own_k, (((1,), (1,)), ((), ())), preferred_element_type=jnp.float32
            )
            row = lax.rem(lax.broadcasted_iota(jnp.int32, own.shape, 0), each)
            col = lax.broadcasted_iota(jnp.int32, own.shape, 1)
            own = jnp.where((row // STEPS == col // STEPS) & (col <= row), own, -1e30)
            s_ref[:, PROMPT:] = own
            top = own
        if do[1]:
            peak = old_peak[...]
        if do[2]:
            own_v = flat(own_ref, tile - 2, base + HEAD)
            lane = lax.broadcasted_iota(jnp.int32, own_v.shape, 1)
            own_v = jnp.concatenate([own_v, jnp.where(lane == 0, 1.0, 0.0)], axis=1)
            own_v = jnp.concatenate([own_v, jnp.zeros_like(own_v)], axis=0).astype(jnp.bfloat16)
            acc = jnp.dot(old_p[:, PROMPT:], own_v, preferred_element_type=jnp.float32)
        for first in range(0, PROMPT, block_cols):
            part = slice(first, first + block_cols)
            if do[0]:
                scores = jnp.dot(query, kt_ref[:, part], preferred_element_type=jnp.float32)
                s_ref[:, part] = scores
                for lane in range(0, block_cols, HEAD):
                    top = jnp.maximum(top, scores[:, lane : lane + HEAD])
            if do[1]:
                for at in range(first, first + block_cols, HEAD):
                    new_p[:, at : at + HEAD] = weights(old_s[:, at : at + HEAD], peak)
            if do[2] and first % 1024 == 0:
                wide = slice(first, first + 1024)
                acc = acc + jnp.dot(
                    old_p[:, wide], ve_ref[wide, :], preferred_element_type=jnp.float32
                )
        if do[1]:
            new_p[:, PROMPT:] = weights(old_s[:, PROMPT:], peak)
        if do[0]:
            peak_ref[...] = jnp.broadcast_to(jnp.max(top, axis=1, keepdims=True), top.shape)
        if do[2]:
            out = acc[:, 0:HEAD] / acc[:, HEAD : HEAD + 1]
            for h in range(heads):
                out_ref[pl.ds((start + tile - 2) * TILE, TILE), :, h * HEAD : (h + 1) * HEAD] = (
                    out[h * each : (h + 1) * each].reshape(TILE, STEPS, HEAD).astype(jnp.bfloat16)
                )

    stages(0, 0, (True, False, False))
    stages(1, 1, (True, True, False))

    @pl.loop(1, tiles // 2)
    def _(pair):
        stages(2 * pair, 0, (True, True, True))
        stages(2 * pair + 1, 1, (True, True, True))

    stages(tiles, 0, (False, True, True))
    stages(tiles + 1, 1, (False, False, True))


def attend(heads, queries, own, keys, values, start, slots, before=(), cols=256):
    assert heads * TILE * STEPS == ROWS
    inputs = [queries, own, keys, values, *before]
    return pl.pallas_call(
        functools.partial(attend_kernel, heads, start // TILE, slots // TILE, cols),
        out_shape=jax.ShapeDtypeStruct((start + slots, STEPS, heads * HEAD), jnp.bfloat16),
        in_specs=[vmem()] * (4 + len(before)),
        out_specs=vmem(),
        scratch_shapes=[pltpu.VMEM((ROWS, PROMPT + HEAD), jnp.float32)] * 2
        + [pltpu.VMEM((ROWS, PROMPT + HEAD), jnp.bfloat16)] * 2
        + [pltpu.VMEM((ROWS, HEAD), jnp.float32)] * 2,
        compiler_params=pltpu.CompilerParams(vmem_limit_bytes=24 * 2**20),
        cost_estimate=pl.CostEstimate(
            flops=4 * slots * STEPS * heads * PROMPT * HEAD,
            bytes_accessed=4 * 2**20,
            transcendentals=slots * STEPS * heads * PROMPT,
        ),
        name="attend",
    )(*inputs)


def project_kernel(first, *refs):
    parts, refs = refs[: RING + 1], refs[RING + 1 :]
    before, refs = (refs[0], refs[1:]) if first else (None, refs)
    weight, out_ref, w_ref, acc_ref, sems = refs
    rows, width = parts[0].shape
    copies = {}
    order = (0, 1, 7, 2, 6, 3, 5, 4)
    for d in order:
        for r in range(4):
            copy = pltpu.make_async_copy(
                weight.at[(d - 4 * (r % 2)) % RING * 4 + r, pl.ds(first, width), :],
                w_ref.at[d, :, pl.ds(r * 256, 256)],
                sems.at[d, r],
            )
            copy.start()
            copies[d, r] = copy
    near = dict(zip((0, 1, 2, 3, 5, 6, 7), parts))
    for d in order:
        for r in range(4):
            copies[d, r].wait()
        if d == 4:
            left = jnp.concatenate([parts[RING - 1][...], parts[RING][...]], axis=0)
        else:
            left = near[d][...]
        for cols in (slice(0, 512), slice(512, 1024)):
            acc = jnp.dot(left, w_ref[d, :, cols], preferred_element_type=jnp.float32)
            if d != order[0]:
                acc = acc + acc_ref[:, cols]
            elif before is not None:
                acc = acc + before[:, cols]
            if d != order[-1]:
                acc_ref[:, cols] = acc
            else:
                out_ref[:, cols] = acc.astype(out_ref.dtype)


def project(parts, before, weight, first):
    rows, width = parts[0].shape
    last = first + width == HEADS * HEAD
    operands = list(parts) + ([before] if before is not None else [])
    return pl.pallas_call(
        functools.partial(project_kernel, first),
        out_shape=jax.ShapeDtypeStruct((rows, 1024), jnp.bfloat16 if last else jnp.float32),
        in_specs=[vmem()] * len(operands) + [hbm()],
        out_specs=vmem(),
        scratch_shapes=[
            pltpu.VMEM((RING, width, 1024), jnp.bfloat16),
            pltpu.VMEM((rows, 1024), jnp.float32),
            pltpu.SemaphoreType.DMA((RING, 4)),
        ],
        compiler_params=pltpu.CompilerParams(vmem_limit_bytes=50 * 2**20),
        cost_estimate=pl.CostEstimate(
            flops=2 * rows * 1024 * RING * width,
            bytes_accessed=RING * width * 1024 * 2 + rows * RING * width * 2,
            transcendentals=0,
        ),
        name="project",
    )(*operands, weight)


def hop(up, down):
    ahead = [(i, (i + 1) % RING) for i in range(RING)]
    back = [((i + 1) % RING, i) for i in range(RING)]
    return lax.ppermute(up, "z", ahead), lax.ppermute(down, "z", back)


def last_hop(up, down):
    half = up.shape[0] // 2
    return hop(up[:half], down[half:])


def exchange(block):
    shape = block.shape
    sent = block.reshape((GROUPS, SLOT) + shape[1:])
    got = lax.all_to_all(sent, GROUP, split_axis=0, concat_axis=0, tiled=True)
    return got.reshape(shape)


def weight_home():
    pairs = []
    for y in range(4):
        for x in range(4):
            for c in range(2):
                for z in range(RING):
                    to_z = y * 2 + x // 2
                    k = (z - to_z - 4 * c) % RING
                    to_y, to_x = k // 2, (k % 2) * 2 + x % 2
                    source = ((y * 4 + x) * 2 + c) * RING + z
                    pairs.append((source, ((to_y * 4 + to_x) * 2 + c) * RING + to_z))
    return pairs


def shards(owner, cont_q, own_keys, own_values, prompt_keys, prompt_values, out_weight):
    turned = lax.ppermute(out_weight, GROUP + ("z",), weight_home())
    packed = pack(owner, cont_q, own_keys, own_values)
    received = [exchange(block) for block in packed]
    turned, received[0] = lax.optimization_barrier((turned, received[0]))
    weight = lax.all_gather(turned, GROUP, axis=0)
    keys, values = prompt_ready(prompt_keys, prompt_values, packed[0])
    slots = GROUPS * SLOT
    rows = HOST * STEPS
    own = received[0]

    tie = lax.optimization_barrier
    attn = attend(PARTS[0], received[0], own, keys, values, 0, slots, cols=512)
    home = unpack(owner, exchange(attn)).reshape(rows, PARTS[0] * HEAD)
    query, home = tie((received[1], home))
    up_1, down_1 = hop(home, home)
    attn = attend(PARTS[1], query, own, keys, values, 0, slots // 2, cols=1024)
    attn, up_1, down_1 = tie((attn, up_1, down_1))
    up_2, down_2 = hop(up_1, down_1)
    attn = attend(PARTS[1], query, own, keys, values, slots // 2, slots // 2, (attn,), cols=1024)
    attn, up_2, down_2 = tie((attn, up_2, down_2))
    up_3, down_3 = hop(up_2, down_2)
    far = last_hop(up_3, down_3)
    first = (home, down_1, down_2, down_3, up_3, up_2, up_1) + far

    home = unpack(owner, exchange(attn)).reshape(rows, PARTS[1] * HEAD)
    up_1, down_1 = hop(home, home)
    up_2, down_2 = hop(up_1, down_1)
    up_3, down_3 = hop(up_2, down_2)
    far = last_hop(up_3, down_3)
    second = (home, down_1, down_2, down_3, up_3, up_2, up_1) + far
    result = project(first, None, weight, 0)
    return project(second, result, weight, PARTS[0] * HEAD)


def solution(mesh):
    mesh = Mesh(mesh.devices.reshape(4, 4, 2, 8), ("y", "x", "c", "z"))
    in_specs = (
        P(GROUP, None),
        P(GROUP, None, "z"),
        P(GROUP, None, "z"),
        P(GROUP, None, "z"),
        P(GROUP, None, "z"),
        P(GROUP, None, "z"),
        P("z", GROUP),
    )
    return jax.shard_map(
        shards, mesh=mesh, in_specs=in_specs, out_specs=P(GROUP, "z"), check_vma=False
    )
```

```python
import functools

import jax
import jax.numpy as jnp
from jax import lax
from jax.experimental import pallas as pl
from jax.experimental.pallas import tpu as pltpu
from jax.sharding import Mesh, PartitionSpec as P

HEAD = 128
GROUPS = 32
SLOT = 2
HOST = 32
STEPS = 8
HEADS = 8
PROMPT = 4096
RING = 8
GROUP = ("y", "x", "c")
PARTS = (4, 4)
SCALE2 = HEAD**-0.5 * 1.4426950408889634


def smem():
    return pl.BlockSpec(memory_space=pltpu.SMEM)


def vmem():
    return pl.BlockSpec(memory_space=pltpu.VMEM)


def hbm():
    return pl.BlockSpec(memory_space=pl.ANY)


def each_place(owner_ref, used_ref, act):
    for g in range(GROUPS):
        used_ref[g] = 0

    @pl.loop(0, HOST)
    def _(c):
        prompt = owner_ref[c, 0]
        rank = used_ref[prompt]
        used_ref[prompt] = rank + 1
        act(c, prompt * SLOT + rank)


def pack_kernel(owner_ref, q_ref, k_ref, v_ref, out_ref, used_ref):
    out_ref[...] = jnp.zeros_like(out_ref)
    width = HEADS * HEAD

    def act(c, place):
        out_ref[place, :, 0:width] = q_ref[c]
        out_ref[place, :, width : width + HEAD] = k_ref[c]
        out_ref[place, :, width + HEAD :] = v_ref[c]

    each_place(owner_ref, used_ref, act)


def pack(owner, q, k, v):
    return pl.pallas_call(
        pack_kernel,
        out_shape=jax.ShapeDtypeStruct((GROUPS * SLOT, STEPS, (HEADS + 2) * HEAD), jnp.bfloat16),
        in_specs=[smem(), vmem(), vmem(), vmem()],
        out_specs=vmem(),
        scratch_shapes=[pltpu.SMEM((GROUPS,), jnp.int32)],
        compiler_params=pltpu.CompilerParams(vmem_limit_bytes=16 * 2**20),
        name="pack",
    )(owner, q, k, v)


def unpack_kernel(owner_ref, got_ref, out_ref, used_ref):
    def act(c, place):
        out_ref[c] = got_ref[place]

    each_place(owner_ref, used_ref, act)


def unpack(owner, got):
    return pl.pallas_call(
        unpack_kernel,
        out_shape=jax.ShapeDtypeStruct((HOST,) + got.shape[1:], got.dtype),
        in_specs=[smem(), vmem()],
        out_specs=vmem(),
        scratch_shapes=[pltpu.SMEM((GROUPS,), jnp.int32)],
        compiler_params=pltpu.CompilerParams(vmem_limit_bytes=16 * 2**20),
        name="unpack",
    )(owner, got)


def prompt_kernel(k_ref, v_ref, after_ref, kt_hbm, ve_hbm, kt_ref, ve_ref, sems):
    for first in range(0, PROMPT, 512):
        rows = slice(first, first + 512)
        kt_ref[:, rows] = k_ref[0, rows, :].astype(jnp.float32).T.astype(jnp.bfloat16)
    copy_k = pltpu.make_async_copy(kt_ref, kt_hbm, sems.at[0])
    copy_k.start()
    for first in range(0, PROMPT, 512):
        rows = slice(first, first + 512)
        ve_ref[rows, 0:HEAD] = v_ref[0, rows, :]
        lane = lax.broadcasted_iota(jnp.int32, (512, HEAD), 1)
        ve_ref[rows, HEAD:] = jnp.where(lane == 0, 1.0, 0.0).astype(jnp.bfloat16)
    copy_v = pltpu.make_async_copy(ve_ref, ve_hbm, sems.at[1])
    copy_v.start()
    copy_k.wait()
    copy_v.wait()


def prompt_ready(keys, values, after):
    return pl.pallas_call(
        prompt_kernel,
        out_shape=[
            jax.ShapeDtypeStruct((HEAD, PROMPT), jnp.bfloat16),
            jax.ShapeDtypeStruct((PROMPT, 2 * HEAD), jnp.bfloat16),
        ],
        in_specs=[vmem(), vmem(), hbm()],
        out_specs=[hbm(), hbm()],
        scratch_shapes=[
            pltpu.VMEM((HEAD, PROMPT), jnp.bfloat16),
            pltpu.VMEM((PROMPT, 2 * HEAD), jnp.bfloat16),
            pltpu.SemaphoreType.DMA((2,)),
        ],
        compiler_params=pltpu.CompilerParams(vmem_limit_bytes=16 * 2**20),
        cost_estimate=pl.CostEstimate(flops=0, bytes_accessed=8 * 2**20, transcendentals=0),
        name="prompt_ready",
    )(keys, values, after)


TILE = 8
ROWS = 256
WIDE = 2048


def attend_kernel(head, heads, start, tiles, q_ref, kt_hbm, ve_hbm, *refs):
    out_ref, kt_ref, ve_ref, sems, *scratch = refs[-10:]
    keys = [
        pltpu.make_async_copy(
            kt_hbm.at[:, pl.ds(first, WIDE)], kt_ref.at[:, pl.ds(first, WIDE)], sems.at[i]
        )
        for i, first in enumerate(range(0, PROMPT, WIDE))
    ]
    values = pltpu.make_async_copy(ve_hbm, ve_ref, sems.at[len(keys)])
    for copy in keys + [values]:
        copy.start()
    if start:
        out_ref[0 : start * TILE] = refs[0][...]
    each = TILE * STEPS
    base = HEADS * HEAD
    s_refs, p_refs, peaks = scratch[0:2], scratch[2:4], scratch[4:6]

    def flat(tile, first):
        block = q_ref[pl.ds((start + tile) * TILE, TILE), :, first : first + HEAD]
        return block.astype(jnp.float32).reshape(each, HEAD)

    def weights(scores, peak):
        return jnp.exp2((scores - peak) * SCALE2).astype(jnp.bfloat16)

    def stages(tile, slot, do):
        s_ref, peak_ref = s_refs[slot], peaks[slot]
        old_s, old_peak, new_p, old_p = s_refs[1 - slot], peaks[1 - slot], p_refs[1 - slot], p_refs[slot]
        top = None
        if do[0]:
            query = jnp.concatenate(
                [flat(tile, (head + h) * HEAD) for h in range(heads)], axis=0
            ).astype(jnp.bfloat16)
            own_k = flat(tile, base)
            own_k = jnp.concatenate([own_k, jnp.zeros_like(own_k)], axis=0).astype(jnp.bfloat16)
            own = lax.dot_general(
                query, own_k, (((1,), (1,)), ((), ())), preferred_element_type=jnp.float32
            )
            row = lax.rem(lax.broadcasted_iota(jnp.int32, own.shape, 0), each)
            col = lax.broadcasted_iota(jnp.int32, own.shape, 1)
            own = jnp.where((row // STEPS == col // STEPS) & (col <= row), own, -1e30)
            s_ref[:, PROMPT:] = own
            top = own
        if do[1]:
            peak = old_peak[...]
        if do[2]:
            own_v = flat(tile - 2, base + HEAD)
            lane = lax.broadcasted_iota(jnp.int32, own_v.shape, 1)
            own_v = jnp.concatenate([own_v, jnp.where(lane == 0, 1.0, 0.0)], axis=1)
            own_v = jnp.concatenate([own_v, jnp.zeros_like(own_v)], axis=0).astype(jnp.bfloat16)
            acc = jnp.dot(old_p[:, PROMPT:], own_v, preferred_element_type=jnp.float32)
        for i, first in enumerate(range(0, PROMPT, WIDE)):
            part = slice(first, first + WIDE)
            if do[0]:
                if not do[1]:
                    keys[i].wait()
                scores = jnp.dot(query, kt_ref[:, part], preferred_element_type=jnp.float32)
                s_ref[:, part] = scores
                for lane in range(0, WIDE, HEAD):
                    top = jnp.maximum(top, scores[:, lane : lane + HEAD])
            if do[1]:
                for at in range(first, first + WIDE, HEAD):
                    new_p[:, at : at + HEAD] = weights(old_s[:, at : at + HEAD], peak)
            if do[2]:
                acc = acc + jnp.dot(
                    old_p[:, part], ve_ref[part, :], preferred_element_type=jnp.float32
                )
        if do[1]:
            new_p[:, PROMPT:] = weights(old_s[:, PROMPT:], peak)
        if do[0]:
            peak_ref[...] = jnp.broadcast_to(jnp.max(top, axis=1, keepdims=True), top.shape)
        if do[2]:
            out = acc[:, 0:HEAD] / acc[:, HEAD : HEAD + 1]
            for h in range(heads):
                out_ref[pl.ds((start + tile - 2) * TILE, TILE), :, h * HEAD : (h + 1) * HEAD] = (
                    out[h * each : (h + 1) * each].reshape(TILE, STEPS, HEAD).astype(jnp.bfloat16)
                )

    stages(0, 0, (True, False, False))
    stages(1, 1, (True, True, False))
    values.wait()

    @pl.loop(1, tiles // 2)
    def _(pair):
        stages(2 * pair, 0, (True, True, True))
        stages(2 * pair + 1, 1, (True, True, True))

    stages(tiles, 0, (False, True, True))
    stages(tiles + 1, 1, (False, False, True))


def attend(head, heads, received, keys, values, start, slots, before=()):
    assert heads * TILE * STEPS == ROWS
    inputs = [received, keys, values, *before]
    return pl.pallas_call(
        functools.partial(attend_kernel, head, heads, start // TILE, slots // TILE),
        out_shape=jax.ShapeDtypeStruct((start + slots, STEPS, heads * HEAD), jnp.bfloat16),
        in_specs=[vmem(), hbm(), hbm()] + [vmem()] * len(before),
        out_specs=vmem(),
        scratch_shapes=[
            pltpu.VMEM(keys.shape, jnp.bfloat16),
            pltpu.VMEM(values.shape, jnp.bfloat16),
            pltpu.SemaphoreType.DMA((PROMPT // WIDE + 1,)),
        ]
        + [pltpu.VMEM((ROWS, PROMPT + HEAD), jnp.float32)] * 2
        + [pltpu.VMEM((ROWS, PROMPT + HEAD), jnp.bfloat16)] * 2
        + [pltpu.VMEM((ROWS, HEAD), jnp.float32)] * 2,
        compiler_params=pltpu.CompilerParams(vmem_limit_bytes=28 * 2**20),
        cost_estimate=pl.CostEstimate(
            flops=4 * slots * STEPS * heads * PROMPT * HEAD,
            bytes_accessed=4 * 2**20,
            transcendentals=slots * STEPS * heads * PROMPT,
        ),
        name="attend",
    )(*inputs)


def project_kernel(first, *refs):
    parts, refs = refs[: RING + 1], refs[RING + 1 :]
    before, refs = (refs[0], refs[1:]) if first else (None, refs)
    weight, out_ref, w_ref, acc_ref, sems = refs
    rows, width = parts[0].shape
    copies = {}
    order = (0, 1, 7, 2, 6, 3, 5, 4)
    for d in order:
        for r in range(4):
            copy = pltpu.make_async_copy(
                weight.at[(d - 4 * (r % 2)) % RING * 4 + r, pl.ds(first, width), :],
                w_ref.at[d, :, pl.ds(r * 256, 256)],
                sems.at[d, r],
            )
            copy.start()
            copies[d, r] = copy
    near = dict(zip((0, 1, 2, 3, 5, 6, 7), parts))
    for d in order:
        for r in range(4):
            copies[d, r].wait()
        if d == 4:
            left = jnp.concatenate([parts[RING - 1][...], parts[RING][...]], axis=0)
        else:
            left = near[d][...]
        for cols in (slice(0, 512), slice(512, 1024)):
            acc = jnp.dot(left, w_ref[d, :, cols], preferred_element_type=jnp.float32)
            if d != order[0]:
                acc = acc + acc_ref[:, cols]
            elif before is not None:
                acc = acc + before[:, cols]
            if d != order[-1]:
                acc_ref[:, cols] = acc
            else:
                out_ref[:, cols] = acc.astype(out_ref.dtype)


def project(parts, before, weight, first):
    rows, width = parts[0].shape
    last = first + width == HEADS * HEAD
    operands = list(parts) + ([before] if before is not None else [])
    return pl.pallas_call(
        functools.partial(project_kernel, first),
        out_shape=jax.ShapeDtypeStruct((rows, 1024), jnp.bfloat16 if last else jnp.float32),
        in_specs=[vmem()] * len(operands) + [hbm()],
        out_specs=vmem(),
        scratch_shapes=[
            pltpu.VMEM((RING, width, 1024), jnp.bfloat16),
            pltpu.VMEM((rows, 1024), jnp.float32),
            pltpu.SemaphoreType.DMA((RING, 4)),
        ],
        compiler_params=pltpu.CompilerParams(vmem_limit_bytes=50 * 2**20),
        cost_estimate=pl.CostEstimate(
            flops=2 * rows * 1024 * RING * width,
            bytes_accessed=RING * width * 1024 * 2 + rows * RING * width * 2,
            transcendentals=0,
        ),
        name="project",
    )(*operands, weight)


def hop(up, down):
    ahead = [(i, (i + 1) % RING) for i in range(RING)]
    back = [((i + 1) % RING, i) for i in range(RING)]
    return lax.ppermute(up, "z", ahead), lax.ppermute(down, "z", back)


def last_hop(up, down):
    half = up.shape[0] // 2
    return hop(up[:half], down[half:])


def exchange(block):
    shape = block.shape
    sent = block.reshape((GROUPS, SLOT) + shape[1:])
    got = lax.all_to_all(sent, GROUP, split_axis=0, concat_axis=0, tiled=True)
    return got.reshape(shape)


def weight_home():
    within, along = [], []
    for y in range(4):
        for x in range(4):
            for c in range(2):
                for z in range(RING):
                    to_z = y * 2 + x // 2
                    k = (z - to_z - 4 * c) % RING
                    group = (y * 4 + x) * 2 + c
                    to_group = (k // 2 * 4 + (k % 2) * 2 + x % 2) * 2 + c
                    within.append((group * RING + z, to_group * RING + z))
                    along.append((to_group * RING + z, to_group * RING + to_z))
    return within, along


def shards(owner, cont_q, own_keys, own_values, prompt_keys, prompt_values, out_weight):
    tie = lax.optimization_barrier
    slots = GROUPS * SLOT
    rows = HOST * STEPS
    within, along = weight_home()
    everyone = GROUP + ("z",)
    turned = lax.ppermute(out_weight, everyone, within)

    packed = pack(owner, cont_q, own_keys, own_values)
    received = exchange(packed)
    keys, values = prompt_ready(prompt_keys, prompt_values, packed)
    turned, keys = tie((turned, keys))
    turned = lax.ppermute(turned, everyone, along)

    attn = attend(0, PARTS[0], received, keys, values, 0, slots)
    turned, attn = tie((turned, attn))
    weight = lax.all_gather(turned, GROUP, axis=0)
    home = unpack(owner, exchange(attn)).reshape(rows, PARTS[0] * HEAD)
    received, home = tie((received, home))
    up_1, down_1 = hop(home, home)
    attn = attend(PARTS[0], PARTS[1], received, keys, values, 0, slots // 2)
    attn, up_1, down_1 = tie((attn, up_1, down_1))
    up_2, down_2 = hop(up_1, down_1)
    attn = attend(PARTS[0], PARTS[1], received, keys, values, slots // 2, slots // 2, (attn,))
    attn, up_2, down_2 = tie((attn, up_2, down_2))
    up_3, down_3 = hop(up_2, down_2)
    far = last_hop(up_3, down_3)
    first = (home, down_1, down_2, down_3, up_3, up_2, up_1) + far

    home = unpack(owner, exchange(attn)).reshape(rows, PARTS[1] * HEAD)
    up_1, down_1 = hop(home, home)
    up_2, down_2 = hop(up_1, down_1)
    up_3, down_3 = hop(up_2, down_2)
    far = last_hop(up_3, down_3)
    second = (home, down_1, down_2, down_3, up_3, up_2, up_1) + far
    result = project(first, None, weight, 0)
    return project(second, result, weight, PARTS[0] * HEAD)


def solution(mesh):
    mesh = Mesh(mesh.devices.reshape(4, 4, 2, 8), ("y", "x", "c", "z"))
    in_specs = (
        P(GROUP, None),
        P(GROUP, None, "z"),
        P(GROUP, None, "z"),
        P(GROUP, None, "z"),
        P(GROUP, None, "z"),
        P(GROUP, None, "z"),
        P("z", GROUP),
    )
    return jax.shard_map(
        shards, mesh=mesh, in_specs=in_specs, out_specs=P(GROUP, "z"), check_vma=False
    )
```

```python
import functools

import jax
import jax.numpy as jnp
from jax import lax
from jax.experimental import pallas as pl
from jax.experimental.pallas import tpu as pltpu
from jax.sharding import Mesh, PartitionSpec as P

HEAD = 128
GROUPS = 32
SLOT = 2
HOST = 32
STEPS = 8
HEADS = 8
PROMPT = 4096
RING = 8
GROUP = ("y", "x", "c")
PARTS = (4, 4)
SCALE2 = HEAD**-0.5 * 1.4426950408889634


def smem():
    return pl.BlockSpec(memory_space=pltpu.SMEM)


def vmem():
    return pl.BlockSpec(memory_space=pltpu.VMEM)


def hbm():
    return pl.BlockSpec(memory_space=pl.ANY)


def each_place(owner_ref, used_ref, act):
    for g in range(GROUPS):
        used_ref[g] = 0

    @pl.loop(0, HOST)
    def _(c):
        prompt = owner_ref[c, 0]
        rank = used_ref[prompt]
        used_ref[prompt] = rank + 1
        act(c, prompt * SLOT + rank)


def pack_kernel(owner_ref, q_ref, k_ref, v_ref, out_ref, used_ref):
    out_ref[...] = jnp.zeros_like(out_ref)
    width = HEADS * HEAD

    def act(c, place):
        out_ref[place, :, 0:width] = q_ref[c]
        out_ref[place, :, width : width + HEAD] = k_ref[c]
        out_ref[place, :, width + HEAD :] = v_ref[c]

    each_place(owner_ref, used_ref, act)


def pack(owner, q, k, v):
    return pl.pallas_call(
        pack_kernel,
        out_shape=jax.ShapeDtypeStruct((GROUPS * SLOT, STEPS, (HEADS + 2) * HEAD), jnp.bfloat16),
        in_specs=[smem(), vmem(), vmem(), vmem()],
        out_specs=vmem(),
        scratch_shapes=[pltpu.SMEM((GROUPS,), jnp.int32)],
        compiler_params=pltpu.CompilerParams(vmem_limit_bytes=16 * 2**20),
        name="pack",
    )(owner, q, k, v)


def unpack_kernel(owner_ref, got_ref, out_ref, used_ref):
    def act(c, place):
        out_ref[c] = got_ref[place]

    each_place(owner_ref, used_ref, act)


def unpack(owner, got):
    return pl.pallas_call(
        unpack_kernel,
        out_shape=jax.ShapeDtypeStruct((HOST,) + got.shape[1:], got.dtype),
        in_specs=[smem(), vmem()],
        out_specs=vmem(),
        scratch_shapes=[pltpu.SMEM((GROUPS,), jnp.int32)],
        compiler_params=pltpu.CompilerParams(vmem_limit_bytes=16 * 2**20),
        name="unpack",
    )(owner, got)


def prompt_kernel(k_ref, v_ref, kt_hbm, ve_hbm, kt_ref, ve_ref, sems):
    for first in range(0, PROMPT, 512):
        rows = slice(first, first + 512)
        kt_ref[:, rows] = k_ref[0, rows, :].astype(jnp.float32).T.astype(jnp.bfloat16)
    copy_k = pltpu.make_async_copy(kt_ref, kt_hbm, sems.at[0])
    copy_k.start()
    for first in range(0, PROMPT, 512):
        rows = slice(first, first + 512)
        ve_ref[rows, 0:HEAD] = v_ref[0, rows, :]
        lane = lax.broadcasted_iota(jnp.int32, (512, HEAD), 1)
        ve_ref[rows, HEAD:] = jnp.where(lane == 0, 1.0, 0.0).astype(jnp.bfloat16)
    copy_v = pltpu.make_async_copy(ve_ref, ve_hbm, sems.at[1])
    copy_v.start()
    copy_k.wait()
    copy_v.wait()


def prompt_ready(keys, values):
    return pl.pallas_call(
        prompt_kernel,
        out_shape=[
            jax.ShapeDtypeStruct((HEAD, PROMPT), jnp.bfloat16),
            jax.ShapeDtypeStruct((PROMPT, 2 * HEAD), jnp.bfloat16),
        ],
        in_specs=[vmem(), vmem()],
        out_specs=[hbm(), hbm()],
        scratch_shapes=[
            pltpu.VMEM((HEAD, PROMPT), jnp.bfloat16),
            pltpu.VMEM((PROMPT, 2 * HEAD), jnp.bfloat16),
            pltpu.SemaphoreType.DMA((2,)),
        ],
        compiler_params=pltpu.CompilerParams(vmem_limit_bytes=58 * 2**20),
        cost_estimate=pl.CostEstimate(flops=0, bytes_accessed=8 * 2**20, transcendentals=0),
        name="prompt_ready",
    )(keys, values)


TILE = 8
ROWS = 256
WIDE = 1024


def attend_kernel(head, heads, start, tiles, q_ref, kt_hbm, ve_hbm, *refs):
    out_ref, kt_ref, ve_ref, sems, *scratch = refs[-10:]
    keys = [
        pltpu.make_async_copy(
            kt_hbm.at[:, pl.ds(first, WIDE)], kt_ref.at[:, pl.ds(first, WIDE)], sems.at[i]
        )
        for i, first in enumerate(range(0, PROMPT, WIDE))
    ]
    values = pltpu.make_async_copy(ve_hbm, ve_ref, sems.at[len(keys)])
    for copy in keys + [values]:
        copy.start()
    if start:
        out_ref[0 : start * TILE] = refs[0][...]
    each = TILE * STEPS
    base = HEADS * HEAD
    s_refs, p_refs, peaks = scratch[0:2], scratch[2:4], scratch[4:6]

    def flat(tile, first):
        block = q_ref[pl.ds((start + tile) * TILE, TILE), :, first : first + HEAD]
        return block.astype(jnp.float32).reshape(each, HEAD)

    def weights(scores, peak):
        return jnp.exp2((scores - peak) * SCALE2).astype(jnp.bfloat16)

    def stages(tile, slot, do):
        s_ref, peak_ref = s_refs[slot], peaks[slot]
        old_s, old_peak, new_p, old_p = s_refs[1 - slot], peaks[1 - slot], p_refs[1 - slot], p_refs[slot]
        top = None
        if do[0]:
            query = jnp.concatenate(
                [flat(tile, (head + h) * HEAD) for h in range(heads)], axis=0
            ).astype(jnp.bfloat16)
            own_k = flat(tile, base)
            own_k = jnp.concatenate([own_k, jnp.zeros_like(own_k)], axis=0).astype(jnp.bfloat16)
            own = lax.dot_general(
                query, own_k, (((1,), (1,)), ((), ())), preferred_element_type=jnp.float32
            )
            row = lax.rem(lax.broadcasted_iota(jnp.int32, own.shape, 0), each)
            col = lax.broadcasted_iota(jnp.int32, own.shape, 1)
            own = jnp.where((row // STEPS == col // STEPS) & (col <= row), own, -1e30)
            s_ref[:, PROMPT:] = own
            top = own
        if do[1]:
            peak = old_peak[...]
        if do[2]:
            own_v = flat(tile - 2, base + HEAD)
            lane = lax.broadcasted_iota(jnp.int32, own_v.shape, 1)
            own_v = jnp.concatenate([own_v, jnp.where(lane == 0, 1.0, 0.0)], axis=1)
            own_v = jnp.concatenate([own_v, jnp.zeros_like(own_v)], axis=0).astype(jnp.bfloat16)
            acc = jnp.dot(old_p[:, PROMPT:], own_v, preferred_element_type=jnp.float32)
        for i, first in enumerate(range(0, PROMPT, WIDE)):
            part = slice(first, first + WIDE)
            if do[0]:
                if not do[1]:
                    keys[i].wait()
                scores = jnp.dot(query, kt_ref[:, part], preferred_element_type=jnp.float32)
                s_ref[:, part] = scores
                for lane in range(0, WIDE, HEAD):
                    top = jnp.maximum(top, scores[:, lane : lane + HEAD])
            if do[1]:
                for at in range(first, first + WIDE, HEAD):
                    new_p[:, at : at + HEAD] = weights(old_s[:, at : at + HEAD], peak)
            if do[2]:
                acc = acc + jnp.dot(
                    old_p[:, part], ve_ref[part, :], preferred_element_type=jnp.float32
                )
        if do[1]:
            new_p[:, PROMPT:] = weights(old_s[:, PROMPT:], peak)
        if do[0]:
            peak_ref[...] = jnp.broadcast_to(jnp.max(top, axis=1, keepdims=True), top.shape)
        if do[2]:
            out = acc[:, 0:HEAD] / acc[:, HEAD : HEAD + 1]
            for h in range(heads):
                out_ref[pl.ds((start + tile - 2) * TILE, TILE), :, h * HEAD : (h + 1) * HEAD] = (
                    out[h * each : (h + 1) * each].reshape(TILE, STEPS, HEAD).astype(jnp.bfloat16)
                )

    stages(0, 0, (True, False, False))
    stages(1, 1, (True, True, False))
    values.wait()

    @pl.loop(1, tiles // 2)
    def _(pair):
        stages(2 * pair, 0, (True, True, True))
        stages(2 * pair + 1, 1, (True, True, True))

    stages(tiles, 0, (False, True, True))
    stages(tiles + 1, 1, (False, False, True))


def attend(head, heads, received, keys, values, start, slots, before=()):
    assert heads * TILE * STEPS == ROWS
    inputs = [received, keys, values, *before]
    return pl.pallas_call(
        functools.partial(attend_kernel, head, heads, start // TILE, slots // TILE),
        out_shape=jax.ShapeDtypeStruct((start + slots, STEPS, heads * HEAD), jnp.bfloat16),
        in_specs=[vmem(), hbm(), hbm()] + [vmem()] * len(before),
        out_specs=vmem(),
        scratch_shapes=[
            pltpu.VMEM(keys.shape, jnp.bfloat16),
            pltpu.VMEM(values.shape, jnp.bfloat16),
            pltpu.SemaphoreType.DMA((PROMPT // WIDE + 1,)),
        ]
        + [pltpu.VMEM((ROWS, PROMPT + HEAD), jnp.float32)] * 2
        + [pltpu.VMEM((ROWS, PROMPT + HEAD), jnp.bfloat16)] * 2
        + [pltpu.VMEM((ROWS, HEAD), jnp.float32)] * 2,
        compiler_params=pltpu.CompilerParams(vmem_limit_bytes=58 * 2**20),
        cost_estimate=pl.CostEstimate(
            flops=4 * slots * STEPS * heads * PROMPT * HEAD,
            bytes_accessed=4 * 2**20,
            transcendentals=slots * STEPS * heads * PROMPT,
        ),
        name="attend",
    )(*inputs)


ORDER = (0, 1, 7, 2, 6, 3, 5, 4)


def weight_copies(weight, w_ref, sems):
    return {
        (d, r): pltpu.make_async_copy(
            weight.at[(d - 4 * (r % 2)) % RING * 4 + r], w_ref.at[d, :, pl.ds(r * 256, 256)], sems.at[d, r]
        )
        for d in ORDER
        for r in range(4)
    }


def fetch_kernel(weight, out_ref, sems):
    copies = weight_copies(weight, out_ref, sems)
    for copy in copies.values():
        copy.start()
    for copy in copies.values():
        copy.wait()


def fetch(weight):
    width = weight.shape[1]
    return pl.pallas_call(
        fetch_kernel,
        out_shape=jax.ShapeDtypeStruct((RING, width, 1024), jnp.bfloat16),
        in_specs=[hbm()],
        out_specs=vmem(),
        scratch_shapes=[pltpu.SemaphoreType.DMA((RING, 4))],
        compiler_params=pltpu.CompilerParams(vmem_limit_bytes=42 * 2**20),
        cost_estimate=pl.CostEstimate(
            flops=0, bytes_accessed=RING * width * 1024 * 4, transcendentals=0
        ),
        name="fetch",
    )(weight)


def project_kernel(places, fetched, *refs):
    parts, refs = refs[: len(places) + (4 in places)], refs[len(places) + (4 in places) :]
    before, refs = (refs[0], refs[1:]) if fetched != "first" else (None, refs)
    if before is None:
        weight, out_ref, w_ref, acc_ref, sems = refs
        copies = weight_copies(weight, w_ref, sems)
        for copy in copies.values():
            copy.start()
    else:
        w_ref, out_ref, acc_ref = refs
    for i, d in enumerate(places):
        if before is None:
            for r in range(4):
                copies[d, r].wait()
        if d == 4:
            left = jnp.concatenate([parts[i][...], parts[i + 1][...]], axis=0)
        else:
            left = parts[i][...]
        for cols in (slice(0, 512), slice(512, 1024)):
            acc = jnp.dot(left, w_ref[d, :, cols], preferred_element_type=jnp.float32)
            if i > 0:
                acc = acc + acc_ref[:, cols]
            elif before is not None:
                acc = acc + before[:, cols]
            if i < len(places) - 1:
                acc_ref[:, cols] = acc
            else:
                out_ref[:, cols] = acc.astype(out_ref.dtype)


def project(places, parts, before, weight, last=False):
    rows, width = parts[0].shape
    start = before is None
    operands = list(parts) + ([] if start else [before])
    scratch = [pltpu.VMEM((rows, 1024), jnp.float32)]
    if start:
        scratch = [pltpu.VMEM((RING, width, 1024), jnp.bfloat16), *scratch, pltpu.SemaphoreType.DMA((RING, 4))]
    return pl.pallas_call(
        functools.partial(project_kernel, places, "first" if start else "later"),
        out_shape=jax.ShapeDtypeStruct((rows, 1024), jnp.bfloat16 if last else jnp.float32),
        in_specs=[vmem()] * len(operands) + [hbm() if start else vmem()],
        out_specs=vmem(),
        scratch_shapes=scratch,
        compiler_params=pltpu.CompilerParams(vmem_limit_bytes=(50 if start else 12) * 2**20),
        cost_estimate=pl.CostEstimate(
            flops=2 * rows * 1024 * len(places) * width,
            bytes_accessed=len(places) * width * 1024 * 2,
            transcendentals=0,
        ),
        name="project",
    )(*operands, weight)


def settle_kernel(in_ref, out_ref):
    out_ref[...] = in_ref[...]


def settle(array):
    return pl.pallas_call(
        settle_kernel,
        out_shape=jax.ShapeDtypeStruct(array.shape, array.dtype),
        in_specs=[vmem()],
        out_specs=vmem(),
        compiler_params=pltpu.CompilerParams(vmem_limit_bytes=8 * 2**20),
        name="settle",
    )(array)


def hop(up, down):
    ahead = [(i, (i + 1) % RING) for i in range(RING)]
    back = [((i + 1) % RING, i) for i in range(RING)]
    return lax.ppermute(up, "z", ahead), lax.ppermute(down, "z", back)


def last_hop(up, down):
    half = up.shape[0] // 2
    return hop(up[:half], down[half:])


def exchange(block):
    shape = block.shape
    sent = block.reshape((GROUPS, SLOT) + shape[1:])
    got = lax.all_to_all(sent, GROUP, split_axis=0, concat_axis=0, tiled=True)
    return got.reshape(shape)


def weight_home():
    within, along = [], []
    for y in range(4):
        for x in range(4):
            for c in range(2):
                for z in range(RING):
                    to_z = y * 2 + x // 2
                    k = (z - to_z - 4 * c) % RING
                    group = (y * 4 + x) * 2 + c
                    to_group = (k // 2 * 4 + (k % 2) * 2 + x % 2) * 2 + c
                    within.append((group * RING + z, to_group * RING + z))
                    along.append((to_group * RING + z, to_group * RING + to_z))
    return within, along


def shards(owner, cont_q, own_keys, own_values, prompt_keys, prompt_values, out_weight):
    tie = lax.optimization_barrier
    slots = GROUPS * SLOT
    rows = HOST * STEPS
    within, along = weight_home()
    everyone = GROUP + ("z",)
    turned = lax.ppermute(out_weight, everyone, within)
    packed = pack(owner, cont_q, own_keys, own_values)
    turned, packed, prompt_keys = tie((turned, packed, prompt_keys))
    turned = lax.ppermute(turned, everyone, along)
    received = exchange(packed)
    keys, values = prompt_ready(prompt_keys, prompt_values)
    turned, received = tie((turned, received))
    width = PARTS[0] * HEAD
    upper = lax.all_gather(turned[:width], GROUP, axis=0)
    lower = lax.all_gather(turned[width:], GROUP, axis=0)

    attn = attend(0, PARTS[0], received, keys, values, 0, slots)
    home = unpack(owner, exchange(attn)).reshape(rows, width)
    received, home = tie((received, home))
    up_1, down_1 = hop(home, home)
    attn = attend(PARTS[0], PARTS[1], received, keys, values, 0, slots // 2)
    attn, up_1, down_1 = tie((attn, up_1, down_1))
    up_2, down_2 = hop(up_1, down_1)
    attn = attend(PARTS[0], PARTS[1], received, keys, values, slots // 2, slots // 2, (attn,))
    attn, up_2, down_2 = tie((attn, up_2, down_2))
    up_3, down_3 = hop(up_2, down_2)
    attn = settle(attn)
    first = (home, down_1, up_1, down_2, up_2, down_3, up_3) + last_hop(up_3, down_3)

    home = unpack(owner, exchange(attn)).reshape(rows, width)
    up_1, down_1 = hop(home, home)
    up_2, down_2 = hop(up_1, down_1)
    result = project(ORDER, first, None, upper)
    result, up_2, down_2 = tie((result, up_2, down_2))
    up_3, down_3 = hop(up_2, down_2)
    lower = fetch(lower)
    lower, up_3, down_3 = tie((lower, up_3, down_3))
    far = last_hop(up_3, down_3)
    result = project(ORDER[:5], (home, down_1, up_1, down_2, up_2), result, lower)
    result, *far = tie((result, *far))
    return project(ORDER[5:], (down_3, up_3, *far), result, lower, last=True)


def solution(mesh):
    mesh = Mesh(mesh.devices.reshape(4, 4, 2, 8), ("y", "x", "c", "z"))
    in_specs = (
        P(GROUP, None),
        P(GROUP, None, "z"),
        P(GROUP, None, "z"),
        P(GROUP, None, "z"),
        P(GROUP, None, "z"),
        P(GROUP, None, "z"),
        P("z", GROUP),
    )
    return jax.shard_map(
        shards, mesh=mesh, in_specs=in_specs, out_specs=P(GROUP, "z"), check_vma=False
    )
```

```python
import functools

import jax
import jax.numpy as jnp
from jax import lax
from jax.experimental import pallas as pl
from jax.experimental.pallas import tpu as pltpu
from jax.sharding import Mesh, PartitionSpec as P

HEAD = 128
GROUPS = 32
SLOT = 2
HOST = 32
STEPS = 8
HEADS = 8
PROMPT = 4096
RING = 8
GROUP = ("y", "x", "c")
PARTS = (4, 4)
SCALE2 = HEAD**-0.5 * 1.4426950408889634


def smem():
    return pl.BlockSpec(memory_space=pltpu.SMEM)


def vmem():
    return pl.BlockSpec(memory_space=pltpu.VMEM)


def hbm():
    return pl.BlockSpec(memory_space=pl.ANY)


def each_place(owner_ref, used_ref, act):
    for g in range(GROUPS):
        used_ref[g] = 0

    @pl.loop(0, HOST)
    def _(c):
        prompt = owner_ref[c, 0]
        rank = used_ref[prompt]
        used_ref[prompt] = rank + 1
        act(c, prompt * SLOT + rank)


def pack_kernel(owner_ref, q_ref, k_ref, v_ref, out_ref, used_ref):
    out_ref[...] = jnp.zeros_like(out_ref)
    width = HEADS * HEAD

    def act(c, place):
        out_ref[place, :, 0:width] = q_ref[c]
        out_ref[place, :, width : width + HEAD] = k_ref[c]
        out_ref[place, :, width + HEAD :] = v_ref[c]

    each_place(owner_ref, used_ref, act)


def pack(owner, q, k, v):
    return pl.pallas_call(
        pack_kernel,
        out_shape=jax.ShapeDtypeStruct((GROUPS * SLOT, STEPS, (HEADS + 2) * HEAD), jnp.bfloat16),
        in_specs=[smem(), vmem(), vmem(), vmem()],
        out_specs=vmem(),
        scratch_shapes=[pltpu.SMEM((GROUPS,), jnp.int32)],
        compiler_params=pltpu.CompilerParams(vmem_limit_bytes=16 * 2**20),
        name="pack",
    )(owner, q, k, v)


def unpack_kernel(owner_ref, got_ref, out_ref, used_ref):
    def act(c, place):
        out_ref[c] = got_ref[place]

    each_place(owner_ref, used_ref, act)


def unpack(owner, got):
    return pl.pallas_call(
        unpack_kernel,
        out_shape=jax.ShapeDtypeStruct((HOST,) + got.shape[1:], got.dtype),
        in_specs=[smem(), vmem()],
        out_specs=vmem(),
        scratch_shapes=[pltpu.SMEM((GROUPS,), jnp.int32)],
        compiler_params=pltpu.CompilerParams(vmem_limit_bytes=16 * 2**20),
        name="unpack",
    )(owner, got)


def prompt_kernel(k_ref, v_ref, kt_ref, ve_ref):
    for first in range(0, PROMPT, 512):
        rows = slice(first, first + 512)
        kt_ref[:, rows] = k_ref[0, rows, :].astype(jnp.float32).T.astype(jnp.bfloat16)
        ve_ref[rows, 0:HEAD] = v_ref[0, rows, :]
        lane = lax.broadcasted_iota(jnp.int32, (512, HEAD), 1)
        ve_ref[rows, HEAD:] = jnp.where(lane == 0, 1.0, 0.0).astype(jnp.bfloat16)


def prompt_ready(keys, values):
    return pl.pallas_call(
        prompt_kernel,
        out_shape=[
            jax.ShapeDtypeStruct((HEAD, PROMPT), jnp.bfloat16),
            jax.ShapeDtypeStruct((PROMPT, 2 * HEAD), jnp.bfloat16),
        ],
        in_specs=[vmem(), vmem()],
        out_specs=[vmem(), vmem()],
        compiler_params=pltpu.CompilerParams(vmem_limit_bytes=12 * 2**20),
        cost_estimate=pl.CostEstimate(flops=0, bytes_accessed=8 * 2**20, transcendentals=0),
        name="prompt_ready",
    )(keys, values)


TILE = 8
ROWS = 256
WIDE = 1024


def attend_kernel(head, heads, start, tiles, q_ref, kt_ref, ve_ref, *refs):
    out_ref, *scratch = refs[-7:]
    if start:
        out_ref[0 : start * TILE] = refs[0][...]
    each = TILE * STEPS
    base = HEADS * HEAD
    s_refs, p_refs, peaks = scratch[0:2], scratch[2:4], scratch[4:6]

    def flat(tile, first):
        block = q_ref[pl.ds((start + tile) * TILE, TILE), :, first : first + HEAD]
        return block.astype(jnp.float32).reshape(each, HEAD)

    def weights(scores, peak):
        return jnp.exp2((scores - peak) * SCALE2).astype(jnp.bfloat16)

    def stages(tile, slot, do):
        s_ref, peak_ref = s_refs[slot], peaks[slot]
        old_s, old_peak, new_p, old_p = s_refs[1 - slot], peaks[1 - slot], p_refs[1 - slot], p_refs[slot]
        top = None
        if do[0]:
            query = jnp.concatenate(
                [flat(tile, (head + h) * HEAD) for h in range(heads)], axis=0
            ).astype(jnp.bfloat16)
            own_k = flat(tile, base)
            own_k = jnp.concatenate([own_k, jnp.zeros_like(own_k)], axis=0).astype(jnp.bfloat16)
            own = lax.dot_general(
                query, own_k, (((1,), (1,)), ((), ())), preferred_element_type=jnp.float32
            )
            row = lax.rem(lax.broadcasted_iota(jnp.int32, own.shape, 0), each)
            col = lax.broadcasted_iota(jnp.int32, own.shape, 1)
            own = jnp.where((row // STEPS == col // STEPS) & (col <= row), own, -1e30)
            s_ref[:, PROMPT:] = own
            top = own
        if do[1]:
            peak = old_peak[...]
        if do[2]:
            own_v = flat(tile - 2, base + HEAD)
            lane = lax.broadcasted_iota(jnp.int32, own_v.shape, 1)
            own_v = jnp.concatenate([own_v, jnp.where(lane == 0, 1.0, 0.0)], axis=1)
            own_v = jnp.concatenate([own_v, jnp.zeros_like(own_v)], axis=0).astype(jnp.bfloat16)
            acc = jnp.dot(old_p[:, PROMPT:], own_v, preferred_element_type=jnp.float32)
        for first in range(0, PROMPT, WIDE):
            part = slice(first, first + WIDE)
            if do[0]:
                scores = jnp.dot(query, kt_ref[:, part], preferred_element_type=jnp.float32)
                s_ref[:, part] = scores
                for lane in range(0, WIDE, HEAD):
                    top = jnp.maximum(top, scores[:, lane : lane + HEAD])
            if do[1]:
                for at in range(first, first + WIDE, HEAD):
                    new_p[:, at : at + HEAD] = weights(old_s[:, at : at + HEAD], peak)
            if do[2]:
                acc = acc + jnp.dot(
                    old_p[:, part], ve_ref[part, :], preferred_element_type=jnp.float32
                )
        if do[1]:
            new_p[:, PROMPT:] = weights(old_s[:, PROMPT:], peak)
        if do[0]:
            peak_ref[...] = jnp.broadcast_to(jnp.max(top, axis=1, keepdims=True), top.shape)
        if do[2]:
            out = acc[:, 0:HEAD] / acc[:, HEAD : HEAD + 1]
            for h in range(heads):
                out_ref[pl.ds((start + tile - 2) * TILE, TILE), :, h * HEAD : (h + 1) * HEAD] = (
                    out[h * each : (h + 1) * each].reshape(TILE, STEPS, HEAD).astype(jnp.bfloat16)
                )

    stages(0, 0, (True, False, False))
    stages(1, 1, (True, True, False))

    @pl.loop(1, tiles // 2)
    def _(pair):
        stages(2 * pair, 0, (True, True, True))
        stages(2 * pair + 1, 1, (True, True, True))

    stages(tiles, 0, (False, True, True))
    stages(tiles + 1, 1, (False, False, True))


def attend(head, heads, received, keys, values, start, slots, before=()):
    assert heads * TILE * STEPS == ROWS
    inputs = [received, keys, values, *before]
    return pl.pallas_call(
        functools.partial(attend_kernel, head, heads, start // TILE, slots // TILE),
        out_shape=jax.ShapeDtypeStruct((start + slots, STEPS, heads * HEAD), jnp.bfloat16),
        in_specs=[vmem()] * len(inputs),
        out_specs=vmem(),
        scratch_shapes=[pltpu.VMEM((ROWS, PROMPT + HEAD), jnp.float32)] * 2
        + [pltpu.VMEM((ROWS, PROMPT + HEAD), jnp.bfloat16)] * 2
        + [pltpu.VMEM((ROWS, HEAD), jnp.float32)] * 2,
        compiler_params=pltpu.CompilerParams(vmem_limit_bytes=24 * 2**20),
        cost_estimate=pl.CostEstimate(
            flops=4 * slots * STEPS * heads * PROMPT * HEAD,
            bytes_accessed=4 * 2**20,
            transcendentals=slots * STEPS * heads * PROMPT,
        ),
        name="attend",
    )(*inputs)


ORDER = (0, 1, 7, 2, 6, 3, 5, 4)


def weight_copies(weight, first, w_ref, sems):
    return {
        (d, r): pltpu.make_async_copy(
            weight.at[(d - 4 * (r % 2)) % RING * 4 + r, pl.ds(first, w_ref.shape[1]), :],
            w_ref.at[d, :, pl.ds(r * 256, 256)],
            sems.at[d, r],
        )
        for d in ORDER
        for r in range(4)
    }


def fetch_kernel(first, weight, out_ref, sems):
    copies = weight_copies(weight, first, out_ref, sems)
    for copy in copies.values():
        copy.start()
    for copy in copies.values():
        copy.wait()


def fetch(weight, first, width):
    return pl.pallas_call(
        functools.partial(fetch_kernel, first),
        out_shape=jax.ShapeDtypeStruct((RING, width, 1024), jnp.bfloat16),
        in_specs=[hbm()],
        out_specs=vmem(),
        scratch_shapes=[pltpu.SemaphoreType.DMA((RING, 4))],
        compiler_params=pltpu.CompilerParams(vmem_limit_bytes=42 * 2**20),
        cost_estimate=pl.CostEstimate(
            flops=0, bytes_accessed=RING * width * 1024 * 4, transcendentals=0
        ),
        name="fetch",
    )(weight)


def project_kernel(places, fetched, *refs):
    parts, refs = refs[: len(places) + (4 in places)], refs[len(places) + (4 in places) :]
    before, refs = (refs[0], refs[1:]) if fetched != "first" else (None, refs)
    if before is None:
        weight, out_ref, w_ref, acc_ref, sems = refs
        copies = weight_copies(weight, 0, w_ref, sems)
        for copy in copies.values():
            copy.start()
    else:
        w_ref, out_ref, acc_ref = refs
    for i, d in enumerate(places):
        if before is None:
            for r in range(4):
                copies[d, r].wait()
        if d == 4:
            left = jnp.concatenate([parts[i][...], parts[i + 1][...]], axis=0)
        else:
            left = parts[i][...]
        for cols in (slice(0, 512), slice(512, 1024)):
            acc = jnp.dot(left, w_ref[d, :, cols], preferred_element_type=jnp.float32)
            if i > 0:
                acc = acc + acc_ref[:, cols]
            elif before is not None:
                acc = acc + before[:, cols]
            if i < len(places) - 1:
                acc_ref[:, cols] = acc
            else:
                out_ref[:, cols] = acc.astype(out_ref.dtype)


def project(places, parts, before, weight, last=False):
    rows, width = parts[0].shape
    start = before is None
    operands = list(parts) + ([] if start else [before])
    scratch = [pltpu.VMEM((rows, 1024), jnp.float32)]
    if start:
        scratch = [pltpu.VMEM((RING, width, 1024), jnp.bfloat16), *scratch, pltpu.SemaphoreType.DMA((RING, 4))]
    return pl.pallas_call(
        functools.partial(project_kernel, places, "first" if start else "later"),
        out_shape=jax.ShapeDtypeStruct((rows, 1024), jnp.bfloat16 if last else jnp.float32),
        in_specs=[vmem()] * len(operands) + [hbm() if start else vmem()],
        out_specs=vmem(),
        scratch_shapes=scratch,
        compiler_params=pltpu.CompilerParams(vmem_limit_bytes=(50 if start else 12) * 2**20),
        cost_estimate=pl.CostEstimate(
            flops=2 * rows * 1024 * len(places) * width,
            bytes_accessed=len(places) * width * 1024 * 2,
            transcendentals=0,
        ),
        name="project",
    )(*operands, weight)


def settle_kernel(in_ref, out_ref):
    out_ref[...] = in_ref[...]


def settle(array):
    return pl.pallas_call(
        settle_kernel,
        out_shape=jax.ShapeDtypeStruct(array.shape, array.dtype),
        in_specs=[vmem()],
        out_specs=vmem(),
        compiler_params=pltpu.CompilerParams(vmem_limit_bytes=8 * 2**20),
        name="settle",
    )(array)


def hop(up, down):
    ahead = [(i, (i + 1) % RING) for i in range(RING)]
    back = [((i + 1) % RING, i) for i in range(RING)]
    return lax.ppermute(up, "z", ahead), lax.ppermute(down, "z", back)


def last_hop(up, down):
    half = up.shape[0] // 2
    return hop(up[:half], down[half:])


def exchange(block):
    shape = block.shape
    sent = block.reshape((GROUPS, SLOT) + shape[1:])
    got = lax.all_to_all(sent, GROUP, split_axis=0, concat_axis=0, tiled=True)
    return got.reshape(shape)


def weight_home():
    within, along = [], []
    for y in range(4):
        for x in range(4):
            for c in range(2):
                for z in range(RING):
                    to_z = y * 2 + x // 2
                    k = (z - to_z - 4 * c) % RING
                    group = (y * 4 + x) * 2 + c
                    to_group = (k // 2 * 4 + (k % 2) * 2 + x % 2) * 2 + c
                    within.append((group * RING + z, to_group * RING + z))
                    along.append((to_group * RING + z, to_group * RING + to_z))
    return within, along


def shards(owner, cont_q, own_keys, own_values, prompt_keys, prompt_values, out_weight):
    tie = lax.optimization_barrier
    slots = GROUPS * SLOT
    rows = HOST * STEPS
    within, along = weight_home()
    everyone = GROUP + ("z",)
    turned = lax.ppermute(out_weight, everyone, within)
    packed = pack(owner, cont_q, own_keys, own_values)
    turned, packed, prompt_keys = tie((turned, packed, prompt_keys))
    turned = lax.ppermute(turned, everyone, along)
    received = exchange(packed)
    keys, values = prompt_ready(prompt_keys, prompt_values)
    width = PARTS[0] * HEAD
    attn = attend(0, PARTS[0], received, keys, values, 0, slots)
    turned, attn = tie((turned, attn))
    weight = lax.all_gather(turned, GROUP, axis=0)
    home = unpack(owner, exchange(attn)).reshape(rows, width)
    received, home = tie((received, home))
    up_1, down_1 = hop(home, home)
    attn = attend(PARTS[0], PARTS[1], received, keys, values, 0, slots // 2)
    attn, up_1, down_1 = tie((attn, up_1, down_1))
    up_2, down_2 = hop(up_1, down_1)
    attn = attend(PARTS[0], PARTS[1], received, keys, values, slots // 2, slots // 2, (attn,))
    attn, up_2, down_2 = tie((attn, up_2, down_2))
    up_3, down_3 = hop(up_2, down_2)
    attn = settle(attn)
    first = (home, down_1, up_1, down_2, up_2, down_3, up_3) + last_hop(up_3, down_3)

    home = unpack(owner, exchange(attn)).reshape(rows, width)
    up_1, down_1 = hop(home, home)
    up_2, down_2 = hop(up_1, down_1)
    result = project(ORDER, first, None, weight)
    result, up_2, down_2 = tie((result, up_2, down_2))
    up_3, down_3 = hop(up_2, down_2)
    lower = fetch(weight, width, PARTS[1] * HEAD)
    lower, up_3, down_3 = tie((lower, up_3, down_3))
    far = last_hop(up_3, down_3)
    result = project(ORDER[:5], (home, down_1, up_1, down_2, up_2), result, lower)
    result, *far = tie((result, *far))
    return project(ORDER[5:], (down_3, up_3, *far), result, lower, last=True)


def solution(mesh):
    mesh = Mesh(mesh.devices.reshape(4, 4, 2, 8), ("y", "x", "c", "z"))
    in_specs = (
        P(GROUP, None),
        P(GROUP, None, "z"),
        P(GROUP, None, "z"),
        P(GROUP, None, "z"),
        P(GROUP, None, "z"),
        P(GROUP, None, "z"),
        P("z", GROUP),
    )
    return jax.shard_map(
        shards, mesh=mesh, in_specs=in_specs, out_specs=P(GROUP, "z"), check_vma=False
    )
```

```python
import functools

import jax
import jax.numpy as jnp
from jax import lax
from jax.experimental import pallas as pl
from jax.experimental.pallas import tpu as pltpu
from jax.sharding import Mesh, PartitionSpec as P

HEAD = 128
GROUPS = 32
SLOT = 2
HOST = 32
STEPS = 8
HEADS = 8
PROMPT = 4096
RING = 8
GROUP = ("y", "x", "c")
PARTS = (4, 4)
SCALE2 = HEAD**-0.5 * 1.4426950408889634


def smem():
    return pl.BlockSpec(memory_space=pltpu.SMEM)


def vmem():
    return pl.BlockSpec(memory_space=pltpu.VMEM)


def hbm():
    return pl.BlockSpec(memory_space=pl.ANY)


def pack_kernel(owner_ref, q_ref, k_ref, v_ref, out_ref, place_ref, used_ref):
    for g in range(GROUPS):
        used_ref[g] = 0
    out_ref[...] = jnp.zeros_like(out_ref)
    width = HEADS * HEAD

    @pl.loop(0, HOST, unroll=4)
    def _(c):
        prompt = owner_ref[c, 0]
        rank = used_ref[prompt]
        used_ref[prompt] = rank + 1
        place = prompt * SLOT + rank
        place_ref[c] = place
        out_ref[place, :, 0:width] = q_ref[c]
        out_ref[place, :, width : width + HEAD] = k_ref[c]
        out_ref[place, :, width + HEAD :] = v_ref[c]


def pack(owner, q, k, v):
    return pl.pallas_call(
        pack_kernel,
        out_shape=[
            jax.ShapeDtypeStruct((GROUPS * SLOT, STEPS, (HEADS + 2) * HEAD), jnp.bfloat16),
            jax.ShapeDtypeStruct((HOST,), jnp.int32),
        ],
        in_specs=[smem(), vmem(), vmem(), vmem()],
        out_specs=[vmem(), smem()],
        scratch_shapes=[pltpu.SMEM((GROUPS,), jnp.int32)],
        compiler_params=pltpu.CompilerParams(vmem_limit_bytes=16 * 2**20),
        name="pack",
    )(owner, q, k, v)


def unpack_kernel(place_ref, got_ref, out_ref):
    for c in range(HOST):
        out_ref[c] = got_ref[place_ref[c]]


def unpack(places, got):
    return pl.pallas_call(
        unpack_kernel,
        out_shape=jax.ShapeDtypeStruct((HOST,) + got.shape[1:], got.dtype),
        in_specs=[smem(), vmem()],
        out_specs=vmem(),
        compiler_params=pltpu.CompilerParams(vmem_limit_bytes=16 * 2**20),
        name="unpack",
    )(places, got)


TILE = 8
ROWS = 256
WIDE = 1024


def attend_kernel(head, heads, start, tiles, fresh, q_ref, k_ref, v_ref, *refs):
    scratch = refs[-6:]
    if fresh:
        out_ref, kt_ref, ve_ref = refs[:3]
        for first in range(0, PROMPT, 512):
            part = slice(first, first + 512)
            kt_ref[:, part] = k_ref[0, part, :].astype(jnp.float32).T.astype(jnp.bfloat16)
            ve_ref[part, 0:HEAD] = v_ref[0, part, :]
            lane = lax.broadcasted_iota(jnp.int32, (512, HEAD), 1)
            ve_ref[part, HEAD:] = jnp.where(lane == 0, 1.0, 0.0).astype(jnp.bfloat16)
    else:
        kt_ref, ve_ref, out_ref = k_ref, v_ref, refs[-7]
    if start:
        out_ref[0 : start * TILE] = refs[0][...]
    each = TILE * STEPS
    base = HEADS * HEAD
    s_refs, p_refs, peaks = scratch[0:2], scratch[2:4], scratch[4:6]

    def flat(tile, first):
        block = q_ref[pl.ds((start + tile) * TILE, TILE), :, first : first + HEAD]
        return block.astype(jnp.float32).reshape(each, HEAD)

    def weights(scores, peak):
        return jnp.exp2((scores - peak) * SCALE2).astype(jnp.bfloat16)

    def stages(tile, slot, do):
        s_ref, peak_ref = s_refs[slot], peaks[slot]
        old_s, old_peak, new_p, old_p = s_refs[1 - slot], peaks[1 - slot], p_refs[1 - slot], p_refs[slot]
        top = None
        if do[0]:
            query = jnp.concatenate(
                [flat(tile, (head + h) * HEAD) for h in range(heads)], axis=0
            ).astype(jnp.bfloat16)
            own_k = flat(tile, base)
            own_k = jnp.concatenate([own_k, jnp.zeros_like(own_k)], axis=0).astype(jnp.bfloat16)
            own = lax.dot_general(
                query, own_k, (((1,), (1,)), ((), ())), preferred_element_type=jnp.float32
            )
            row = lax.rem(lax.broadcasted_iota(jnp.int32, own.shape, 0), each)
            col = lax.broadcasted_iota(jnp.int32, own.shape, 1)
            own = jnp.where((row // STEPS == col // STEPS) & (col <= row), own, -1e30)
            s_ref[:, PROMPT:] = own
            top = own
        if do[1]:
            peak = old_peak[...]
        if do[2]:
            own_v = flat(tile - 2, base + HEAD)
            lane = lax.broadcasted_iota(jnp.int32, own_v.shape, 1)
            own_v = jnp.concatenate([own_v, jnp.where(lane == 0, 1.0, 0.0)], axis=1)
            own_v = jnp.concatenate([own_v, jnp.zeros_like(own_v)], axis=0).astype(jnp.bfloat16)
            acc = jnp.dot(old_p[:, PROMPT:], own_v, preferred_element_type=jnp.float32)
        for first in range(0, PROMPT, WIDE):
            part = slice(first, first + WIDE)
            if do[0]:
                scores = jnp.dot(query, kt_ref[:, part], preferred_element_type=jnp.float32)
                s_ref[:, part] = scores
                for lane in range(0, WIDE, HEAD):
                    top = jnp.maximum(top, scores[:, lane : lane + HEAD])
            if do[1]:
                for at in range(first, first + WIDE, HEAD):
                    new_p[:, at : at + HEAD] = weights(old_s[:, at : at + HEAD], peak)
            if do[2]:
                acc = acc + jnp.dot(
                    old_p[:, part], ve_ref[part, :], preferred_element_type=jnp.float32
                )
        if do[1]:
            new_p[:, PROMPT:] = weights(old_s[:, PROMPT:], peak)
        if do[0]:
            peak_ref[...] = jnp.broadcast_to(jnp.max(top, axis=1, keepdims=True), top.shape)
        if do[2]:
            out = acc[:, 0:HEAD] / acc[:, HEAD : HEAD + 1]
            for h in range(heads):
                out_ref[pl.ds((start + tile - 2) * TILE, TILE), :, h * HEAD : (h + 1) * HEAD] = (
                    out[h * each : (h + 1) * each].reshape(TILE, STEPS, HEAD).astype(jnp.bfloat16)
                )

    stages(0, 0, (True, False, False))
    stages(1, 1, (True, True, False))

    for pair in range(1, tiles // 2):
        stages(2 * pair, 0, (True, True, True))
        stages(2 * pair + 1, 1, (True, True, True))
    stages(tiles, 0, (False, True, True))
    stages(tiles + 1, 1, (False, False, True))


def attend(head, heads, received, keys, values, start, slots, before=(), fresh=False):
    assert heads * TILE * STEPS == ROWS
    inputs = [received, keys, values, *before]
    outs = [jax.ShapeDtypeStruct((start + slots, STEPS, heads * HEAD), jnp.bfloat16)]
    if fresh:
        outs.append(jax.ShapeDtypeStruct((HEAD, PROMPT), jnp.bfloat16))
        outs.append(jax.ShapeDtypeStruct((PROMPT, 2 * HEAD), jnp.bfloat16))
    return pl.pallas_call(
        functools.partial(attend_kernel, head, heads, start // TILE, slots // TILE, fresh),
        out_shape=outs,
        in_specs=[vmem()] * len(inputs),
        out_specs=[vmem()] * len(outs),
        scratch_shapes=[pltpu.VMEM((ROWS, PROMPT + HEAD), jnp.float32)] * 2
        + [pltpu.VMEM((ROWS, PROMPT + HEAD), jnp.bfloat16)] * 2
        + [pltpu.VMEM((ROWS, HEAD), jnp.float32)] * 2,
        compiler_params=pltpu.CompilerParams(vmem_limit_bytes=24 * 2**20),
        cost_estimate=pl.CostEstimate(
            flops=4 * slots * STEPS * heads * PROMPT * HEAD,
            bytes_accessed=4 * 2**20,
            transcendentals=slots * STEPS * heads * PROMPT,
        ),
        name="attend",
    )(*inputs)


ORDER = (0, 1, 7, 2, 6, 3, 5, 4)


def weight_copies(plane, weight, first, w_ref, sems):
    return {
        (d, r): pltpu.make_async_copy(
            weight.at[lax.rem(2 * plane + d + 5 * (r % 2), RING) * 4 + r, pl.ds(first, w_ref.shape[1]), :],
            w_ref.at[d, :, pl.ds(r * 256, 256)],
            sems.at[d, r],
        )
        for d in ORDER
        for r in range(4)
    }


def fetch_kernel(first, plane_ref, weight, out_ref, sems):
    copies = weight_copies(plane_ref[0], weight, first, out_ref, sems)
    for copy in copies.values():
        copy.start()
    for copy in copies.values():
        copy.wait()


def fetch(plane, weight, first, width):
    return pl.pallas_call(
        functools.partial(fetch_kernel, first),
        out_shape=jax.ShapeDtypeStruct((RING, width, 1024), jnp.bfloat16),
        in_specs=[smem(), hbm()],
        out_specs=vmem(),
        scratch_shapes=[pltpu.SemaphoreType.DMA((RING, 4))],
        compiler_params=pltpu.CompilerParams(vmem_limit_bytes=42 * 2**20),
        cost_estimate=pl.CostEstimate(
            flops=0, bytes_accessed=RING * width * 1024 * 4, transcendentals=0
        ),
        name="fetch",
    )(plane, weight)


def project_kernel(places, fetched, plane_ref, *refs):
    parts, refs = refs[: len(places) + (4 in places)], refs[len(places) + (4 in places) :]
    before, refs = (refs[0], refs[1:]) if fetched != "first" else (None, refs)
    if before is None:
        weight, out_ref, w_ref, acc_ref, sems = refs
        copies = weight_copies(plane_ref[0], weight, 0, w_ref, sems)
        for copy in copies.values():
            copy.start()
    else:
        w_ref, out_ref, acc_ref = refs
    for i, d in enumerate(places):
        if before is None:
            for r in range(4):
                copies[d, r].wait()
        if d == 4:
            left = jnp.concatenate([parts[i][...], parts[i + 1][...]], axis=0)
        else:
            left = parts[i][...]
        for cols in (slice(0, 512), slice(512, 1024)):
            acc = jnp.dot(left, w_ref[d, :, cols], preferred_element_type=jnp.float32)
            if i > 0:
                acc = acc + acc_ref[:, cols]
            elif before is not None:
                acc = acc + before[:, cols]
            if i < len(places) - 1:
                acc_ref[:, cols] = acc
            else:
                out_ref[:, cols] = acc.astype(out_ref.dtype)


def project(places, plane, parts, before, weight, last=False):
    rows, width = parts[0].shape
    start = before is None
    operands = list(parts) + ([] if start else [before])
    scratch = [pltpu.VMEM((rows, 1024), jnp.float32)]
    if start:
        scratch = [pltpu.VMEM((RING, width, 1024), jnp.bfloat16), *scratch, pltpu.SemaphoreType.DMA((RING, 4))]
    return pl.pallas_call(
        functools.partial(project_kernel, places, "first" if start else "later"),
        out_shape=jax.ShapeDtypeStruct((rows, 1024), jnp.bfloat16 if last else jnp.float32),
        in_specs=[smem()] + [vmem()] * len(operands) + [hbm() if start else vmem()],
        out_specs=vmem(),
        scratch_shapes=scratch,
        compiler_params=pltpu.CompilerParams(vmem_limit_bytes=(50 if start else 12) * 2**20),
        cost_estimate=pl.CostEstimate(
            flops=2 * rows * 1024 * len(places) * width,
            bytes_accessed=len(places) * width * 1024 * 2,
            transcendentals=0,
        ),
        name="project",
    )(plane, *operands, weight)


def settle_kernel(in_ref, out_ref):
    out_ref[...] = in_ref[...]


def settle(array):
    return pl.pallas_call(
        settle_kernel,
        out_shape=jax.ShapeDtypeStruct(array.shape, array.dtype),
        in_specs=[vmem()],
        out_specs=vmem(),
        compiler_params=pltpu.CompilerParams(vmem_limit_bytes=8 * 2**20),
        name="settle",
    )(array)


def hop(up, down):
    ahead = [(i, (i + 1) % RING) for i in range(RING)]
    back = [((i + 1) % RING, i) for i in range(RING)]
    return lax.ppermute(up, "z", ahead), lax.ppermute(down, "z", back)


def last_hop(up, down):
    half = up.shape[0] // 2
    return hop(up[:half], down[half:])


def exchange(block):
    shape = block.shape
    sent = block.reshape((GROUPS, SLOT) + shape[1:])
    got = lax.all_to_all(sent, GROUP, split_axis=0, concat_axis=0, tiled=True)
    return got.reshape(shape)


def weight_home():
    within, along = [], []
    for y in range(4):
        for x in range(4):
            for c in range(2):
                for z in range(RING):
                    to_z = y * 2 + x // 2
                    k = (z + to_z + 5 * c) % RING
                    group = (y * 4 + x) * 2 + c
                    to_group = (k // 2 * 4 + (k % 2) * 2 + x % 2) * 2 + c
                    within.append((group * RING + z, to_group * RING + z))
                    along.append((to_group * RING + z, to_group * RING + to_z))
    return within, along


def shards(owner, cont_q, own_keys, own_values, prompt_keys, prompt_values, out_weight):
    tie = lax.optimization_barrier
    slots = GROUPS * SLOT
    rows = HOST * STEPS
    within, along = weight_home()
    everyone = GROUP + ("z",)
    plane = lax.axis_index("z").astype(jnp.int32).reshape(1)
    turned = lax.ppermute(out_weight, everyone, within)
    packed, places = pack(owner, cont_q, own_keys, own_values)
    turned, packed = tie((turned, packed))
    turned = lax.ppermute(turned, everyone, along)
    received = exchange(packed)
    turned, received = tie((turned, received))
    weight = lax.all_gather(turned, GROUP, axis=0)

    width = PARTS[0] * HEAD
    attn, keys, values = attend(
        0, PARTS[0], received, prompt_keys, prompt_values, 0, slots, fresh=True
    )
    home = unpack(places, exchange(attn)).reshape(rows, width)
    received, home = tie((received, home))
    up_1, down_1 = hop(home, home)
    (attn,) = attend(PARTS[0], PARTS[1], received, keys, values, 0, slots // 2)
    attn, up_1, down_1 = tie((attn, up_1, down_1))
    up_2, down_2 = hop(up_1, down_1)
    (attn,) = attend(PARTS[0], PARTS[1], received, keys, values, slots // 2, slots // 2, (attn,))
    attn, up_2, down_2 = tie((attn, up_2, down_2))
    up_3, down_3 = hop(up_2, down_2)
    attn = settle(attn)
    first = (home, down_1, up_1, down_2, up_2, down_3, up_3) + last_hop(up_3, down_3)

    home = unpack(places, exchange(attn)).reshape(rows, width)
    up_1, down_1 = hop(home, home)
    up_2, down_2 = hop(up_1, down_1)
    result = project(ORDER, plane, first, None, weight)
    result, up_2, down_2 = tie((result, up_2, down_2))
    up_3, down_3 = hop(up_2, down_2)
    lower = fetch(plane, weight, width, PARTS[1] * HEAD)
    lower, up_3, down_3 = tie((lower, up_3, down_3))
    far = last_hop(up_3, down_3)
    result = project(ORDER[:5], plane, (home, down_1, up_1, down_2, up_2), result, lower)
    result, *far = tie((result, *far))
    return project(ORDER[5:], plane, (down_3, up_3, *far), result, lower, last=True)


def solution(mesh):
    mesh = Mesh(mesh.devices.reshape(4, 4, 2, 8), ("y", "x", "c", "z"))
    in_specs = (
        P(GROUP, None),
        P(GROUP, None, "z"),
        P(GROUP, None, "z"),
        P(GROUP, None, "z"),
        P(GROUP, None, "z"),
        P(GROUP, None, "z"),
        P("z", GROUP),
    )
    return jax.shard_map(
        shards, mesh=mesh, in_specs=in_specs, out_specs=P(GROUP, "z"), check_vma=False
    )
```

```python
import functools

import jax
import jax.numpy as jnp
from jax import lax
from jax.experimental import pallas as pl
from jax.experimental.pallas import tpu as pltpu
from jax.sharding import Mesh, PartitionSpec as P

HEAD = 128
GROUPS = 32
SLOT = 2
HOST = 32
STEPS = 8
HEADS = 8
PROMPT = 4096
RING = 8
GROUP = ("y", "x", "c")
PARTS = (4, 4)
SCALE2 = HEAD**-0.5 * 1.4426950408889634


def smem():
    return pl.BlockSpec(memory_space=pltpu.SMEM)


def vmem():
    return pl.BlockSpec(memory_space=pltpu.VMEM)


def hbm():
    return pl.BlockSpec(memory_space=pl.ANY)


def pack_kernel(owner_ref, q_ref, k_ref, v_ref, out_ref, place_ref, used_ref):
    for g in range(GROUPS):
        used_ref[g] = 0
    out_ref[...] = jnp.zeros_like(out_ref)
    width = HEADS * HEAD

    @pl.loop(0, HOST, unroll=4)
    def _(c):
        prompt = owner_ref[c, 0]
        rank = used_ref[prompt]
        used_ref[prompt] = rank + 1
        place = prompt * SLOT + rank
        place_ref[c] = place
        out_ref[place, :, 0:width] = q_ref[c]
        out_ref[place, :, width : width + HEAD] = k_ref[c]
        out_ref[place, :, width + HEAD :] = v_ref[c]


def pack(owner, q, k, v):
    return pl.pallas_call(
        pack_kernel,
        out_shape=[
            jax.ShapeDtypeStruct((GROUPS * SLOT, STEPS, (HEADS + 2) * HEAD), jnp.bfloat16),
            jax.ShapeDtypeStruct((HOST,), jnp.int32),
        ],
        in_specs=[smem(), vmem(), vmem(), vmem()],
        out_specs=[vmem(), smem()],
        scratch_shapes=[pltpu.SMEM((GROUPS,), jnp.int32)],
        compiler_params=pltpu.CompilerParams(vmem_limit_bytes=16 * 2**20),
        name="pack",
    )(owner, q, k, v)


def unpack_kernel(place_ref, got_ref, out_ref):
    for c in range(HOST):
        out_ref[c] = got_ref[place_ref[c]]


def unpack(places, got):
    return pl.pallas_call(
        unpack_kernel,
        out_shape=jax.ShapeDtypeStruct((HOST,) + got.shape[1:], got.dtype),
        in_specs=[smem(), vmem()],
        out_specs=vmem(),
        compiler_params=pltpu.CompilerParams(vmem_limit_bytes=16 * 2**20),
        name="unpack",
    )(places, got)


TILE = 8
ROWS = 256
WIDE = 1024


def attend_kernel(head, heads, start, tiles, fresh, q_ref, k_ref, v_ref, *refs):
    scratch = refs[-6:]
    if fresh:
        out_ref, kt_ref, ve_ref = refs[:3]
        for first in range(0, PROMPT, 512):
            part = slice(first, first + 512)
            kt_ref[:, part] = k_ref[0, part, :].astype(jnp.float32).T.astype(jnp.bfloat16)
            ve_ref[part, 0:HEAD] = v_ref[0, part, :]
            lane = lax.broadcasted_iota(jnp.int32, (512, HEAD), 1)
            ve_ref[part, HEAD:] = jnp.where(lane == 0, 1.0, 0.0).astype(jnp.bfloat16)
    else:
        kt_ref, ve_ref, out_ref = k_ref, v_ref, refs[-7]
    if start:
        out_ref[0 : start * TILE] = refs[0][...]
    each = TILE * STEPS
    base = HEADS * HEAD
    s_refs, p_refs, peaks = scratch[0:2], scratch[2:4], scratch[4:6]

    def flat(tile, first):
        block = q_ref[pl.ds((start + tile) * TILE, TILE), :, first : first + HEAD]
        return block.astype(jnp.float32).reshape(each, HEAD)

    def weights(scores, peak):
        return jnp.exp2((scores - peak) * SCALE2).astype(jnp.bfloat16)

    def stages(tile, slot, do):
        s_ref, peak_ref = s_refs[slot], peaks[slot]
        old_s, old_peak, new_p, old_p = s_refs[1 - slot], peaks[1 - slot], p_refs[1 - slot], p_refs[slot]
        top = None
        if do[0]:
            query = jnp.concatenate(
                [flat(tile, (head + h) * HEAD) for h in range(heads)], axis=0
            ).astype(jnp.bfloat16)
            own_k = flat(tile, base)
            own_k = jnp.concatenate([own_k, jnp.zeros_like(own_k)], axis=0).astype(jnp.bfloat16)
            own = lax.dot_general(
                query, own_k, (((1,), (1,)), ((), ())), preferred_element_type=jnp.float32
            )
            row = lax.rem(lax.broadcasted_iota(jnp.int32, own.shape, 0), each)
            col = lax.broadcasted_iota(jnp.int32, own.shape, 1)
            own = jnp.where((row // STEPS == col // STEPS) & (col <= row), own, -1e30)
            s_ref[:, PROMPT:] = own
            top = own
        if do[1]:
            peak = old_peak[...]
        if do[2]:
            own_v = flat(tile - 2, base + HEAD)
            lane = lax.broadcasted_iota(jnp.int32, own_v.shape, 1)
            own_v = jnp.concatenate([own_v, jnp.where(lane == 0, 1.0, 0.0)], axis=1)
            own_v = jnp.concatenate([own_v, jnp.zeros_like(own_v)], axis=0).astype(jnp.bfloat16)
            acc = jnp.dot(old_p[:, PROMPT:], own_v, preferred_element_type=jnp.float32)
        for first in range(0, PROMPT, WIDE):
            part = slice(first, first + WIDE)
            if do[0]:
                scores = jnp.dot(query, kt_ref[:, part], preferred_element_type=jnp.float32)
                s_ref[:, part] = scores
                for lane in range(0, WIDE, HEAD):
                    top = jnp.maximum(top, scores[:, lane : lane + HEAD])
            if do[1]:
                for at in range(first, first + WIDE, HEAD):
                    new_p[:, at : at + HEAD] = weights(old_s[:, at : at + HEAD], peak)
            if do[2]:
                acc = acc + jnp.dot(
                    old_p[:, part], ve_ref[part, :], preferred_element_type=jnp.float32
                )
        if do[1]:
            new_p[:, PROMPT:] = weights(old_s[:, PROMPT:], peak)
        if do[0]:
            peak_ref[...] = jnp.broadcast_to(jnp.max(top, axis=1, keepdims=True), top.shape)
        if do[2]:
            out = acc[:, 0:HEAD] / acc[:, HEAD : HEAD + 1]
            for h in range(heads):
                out_ref[pl.ds((start + tile - 2) * TILE, TILE), :, h * HEAD : (h + 1) * HEAD] = (
                    out[h * each : (h + 1) * each].reshape(TILE, STEPS, HEAD).astype(jnp.bfloat16)
                )

    stages(0, 0, (True, False, False))
    stages(1, 1, (True, True, False))

    for pair in range(1, tiles // 2):
        stages(2 * pair, 0, (True, True, True))
        stages(2 * pair + 1, 1, (True, True, True))
    stages(tiles, 0, (False, True, True))
    stages(tiles + 1, 1, (False, False, True))


def attend(head, heads, received, keys, values, start, slots, before=(), fresh=False):
    assert heads * TILE * STEPS == ROWS
    inputs = [received, keys, values, *before]
    outs = [jax.ShapeDtypeStruct((start + slots, STEPS, heads * HEAD), jnp.bfloat16)]
    if fresh:
        outs.append(jax.ShapeDtypeStruct((HEAD, PROMPT), jnp.bfloat16))
        outs.append(jax.ShapeDtypeStruct((PROMPT, 2 * HEAD), jnp.bfloat16))
    return pl.pallas_call(
        functools.partial(attend_kernel, head, heads, start // TILE, slots // TILE, fresh),
        out_shape=outs,
        in_specs=[vmem()] * len(inputs),
        out_specs=[vmem()] * len(outs),
        scratch_shapes=[pltpu.VMEM((ROWS, PROMPT + HEAD), jnp.float32)] * 2
        + [pltpu.VMEM((ROWS, PROMPT + HEAD), jnp.bfloat16)] * 2
        + [pltpu.VMEM((ROWS, HEAD), jnp.float32)] * 2,
        compiler_params=pltpu.CompilerParams(vmem_limit_bytes=24 * 2**20),
        cost_estimate=pl.CostEstimate(
            flops=4 * slots * STEPS * heads * PROMPT * HEAD,
            bytes_accessed=4 * 2**20,
            transcendentals=slots * STEPS * heads * PROMPT,
        ),
        name="attend",
    )(*inputs)


ORDER = (0, 1, 7, 2, 6, 3, 5, 4)


def weight_copies(plane, weight, first, w_ref, sems):
    return {
        (d, r): pltpu.make_async_copy(
            weight.at[lax.rem(2 * plane + d + 5 * (r % 2), RING) * 4 + r, pl.ds(first, w_ref.shape[1]), :],
            w_ref.at[d, :, pl.ds(r * 256, 256)],
            sems.at[d, r],
        )
        for d in ORDER
        for r in range(4)
    }


def fetch_kernel(first, plane_ref, weight, out_ref, sems):
    copies = weight_copies(plane_ref[0], weight, first, out_ref, sems)
    for copy in copies.values():
        copy.start()
    for copy in copies.values():
        copy.wait()


def fetch(plane, weight, first, width):
    return pl.pallas_call(
        functools.partial(fetch_kernel, first),
        out_shape=jax.ShapeDtypeStruct((RING, width, 1024), jnp.bfloat16),
        in_specs=[smem(), hbm()],
        out_specs=vmem(),
        scratch_shapes=[pltpu.SemaphoreType.DMA((RING, 4))],
        compiler_params=pltpu.CompilerParams(vmem_limit_bytes=42 * 2**20),
        cost_estimate=pl.CostEstimate(
            flops=0, bytes_accessed=RING * width * 1024 * 4, transcendentals=0
        ),
        name="fetch",
    )(plane, weight)


def project_kernel(places, fetched, plane_ref, *refs):
    parts, refs = refs[: len(places) + (4 in places)], refs[len(places) + (4 in places) :]
    before, refs = (refs[0], refs[1:]) if fetched != "first" else (None, refs)
    if before is None:
        weight, out_ref, w_ref, acc_ref, sems = refs
        copies = weight_copies(plane_ref[0], weight, 0, w_ref, sems)
        for copy in copies.values():
            copy.start()
    else:
        w_ref, out_ref, acc_ref = refs
    for i, d in enumerate(places):
        if before is None:
            for r in range(4):
                copies[d, r].wait()
        if d == 4:
            left = jnp.concatenate([parts[i][...], parts[i + 1][...]], axis=0)
        else:
            left = parts[i][...]
        for cols in (slice(0, 512), slice(512, 1024)):
            acc = jnp.dot(left, w_ref[d, :, cols], preferred_element_type=jnp.float32)
            if i > 0:
                acc = acc + acc_ref[:, cols]
            elif before is not None:
                acc = acc + before[:, cols]
            if i < len(places) - 1:
                acc_ref[:, cols] = acc
            else:
                out_ref[:, cols] = acc.astype(out_ref.dtype)


def project(places, plane, parts, before, weight, last=False):
    rows, width = parts[0].shape
    start = before is None
    operands = list(parts) + ([] if start else [before])
    scratch = [pltpu.VMEM((rows, 1024), jnp.float32)]
    if start:
        scratch = [pltpu.VMEM((RING, width, 1024), jnp.bfloat16), *scratch, pltpu.SemaphoreType.DMA((RING, 4))]
    return pl.pallas_call(
        functools.partial(project_kernel, places, "first" if start else "later"),
        out_shape=jax.ShapeDtypeStruct((rows, 1024), jnp.bfloat16 if last else jnp.float32),
        in_specs=[smem()] + [vmem()] * len(operands) + [hbm() if start else vmem()],
        out_specs=vmem(),
        scratch_shapes=scratch,
        compiler_params=pltpu.CompilerParams(vmem_limit_bytes=(50 if start else 12) * 2**20),
        cost_estimate=pl.CostEstimate(
            flops=2 * rows * 1024 * len(places) * width,
            bytes_accessed=len(places) * width * 1024 * 2,
            transcendentals=0,
        ),
        name="project",
    )(plane, *operands, weight)


def hop(up, down):
    ahead = [(i, (i + 1) % RING) for i in range(RING)]
    back = [((i + 1) % RING, i) for i in range(RING)]
    return lax.ppermute(up, "z", ahead), lax.ppermute(down, "z", back)


def last_hop(up, down):
    half = up.shape[0] // 2
    return hop(up[:half], down[half:])


def exchange(block):
    shape = block.shape
    sent = block.reshape((GROUPS, SLOT) + shape[1:])
    got = lax.all_to_all(sent, GROUP, split_axis=0, concat_axis=0, tiled=True)
    return got.reshape(shape)


def weight_home():
    within, along = [], []
    for y in range(4):
        for x in range(4):
            for c in range(2):
                for z in range(RING):
                    to_z = y * 2 + x // 2
                    k = (z + to_z + 5 * c) % RING
                    group = (y * 4 + x) * 2 + c
                    to_group = (k // 2 * 4 + (k % 2) * 2 + x % 2) * 2 + c
                    within.append((group * RING + z, to_group * RING + z))
                    along.append((to_group * RING + z, to_group * RING + to_z))
    return within, along


def shards(owner, cont_q, own_keys, own_values, prompt_keys, prompt_values, out_weight):
    tie = lax.optimization_barrier
    slots = GROUPS * SLOT
    rows = HOST * STEPS
    within, along = weight_home()
    everyone = GROUP + ("z",)
    plane = lax.axis_index("z").astype(jnp.int32).reshape(1)
    turned = lax.ppermute(out_weight, everyone, within)
    turned, owner = tie((turned, owner))
    turned = lax.ppermute(turned, everyone, along)
    packed, places = pack(owner, cont_q, own_keys, own_values)
    received = exchange(packed)
    turned, received = tie((turned, received))
    weight = lax.all_gather(turned, GROUP, axis=0)

    width = PARTS[0] * HEAD
    attn, keys, values = attend(
        0, PARTS[0], received, prompt_keys, prompt_values, 0, slots, fresh=True
    )
    back = exchange(attn)
    (attn,) = attend(PARTS[0], PARTS[1], received, keys, values, 0, slots)
    back, _ = tie((back, attn))
    home = unpack(places, back).reshape(rows, width)
    back = exchange(attn)
    up_1, down_1 = hop(home, home)
    places, up_1, down_1 = tie((places, up_1, down_1))
    up_2, down_2 = hop(up_1, down_1)
    up_3, down_3 = hop(up_2, down_2)
    first = (home, down_1, up_1, down_2, up_2, down_3, up_3) + last_hop(up_3, down_3)

    home = unpack(places, back).reshape(rows, width)
    up_1, down_1 = hop(home, home)
    up_2, down_2 = hop(up_1, down_1)
    result = project(ORDER, plane, first, None, weight)
    result, up_2, down_2 = tie((result, up_2, down_2))
    up_3, down_3 = hop(up_2, down_2)
    lower = fetch(plane, weight, width, PARTS[1] * HEAD)
    lower, up_3, down_3 = tie((lower, up_3, down_3))
    far = last_hop(up_3, down_3)
    result = project(ORDER[:5], plane, (home, down_1, up_1, down_2, up_2), result, lower)
    result, *far = tie((result, *far))
    return project(ORDER[5:], plane, (down_3, up_3, *far), result, lower, last=True)


def solution(mesh):
    mesh = Mesh(mesh.devices.reshape(4, 4, 2, 8), ("y", "x", "c", "z"))
    in_specs = (
        P(GROUP, None),
        P(GROUP, None, "z"),
        P(GROUP, None, "z"),
        P(GROUP, None, "z"),
        P(GROUP, None, "z"),
        P(GROUP, None, "z"),
        P("z", GROUP),
    )
    return jax.shard_map(
        shards, mesh=mesh, in_specs=in_specs, out_specs=P(GROUP, "z"), check_vma=False
    )
```

```python
import functools

import jax
import jax.numpy as jnp
from jax import lax
from jax.experimental import pallas as pl
from jax.experimental.pallas import tpu as pltpu
from jax.sharding import Mesh, PartitionSpec as P

HEAD = 128
GROUPS = 32
SLOT = 2
HOST = 32
STEPS = 8
HEADS = 8
PROMPT = 4096
RING = 8
GROUP = ("y", "x", "c")
PARTS = (4, 4)
SCALE2 = HEAD**-0.5 * 1.4426950408889634


def smem():
    return pl.BlockSpec(memory_space=pltpu.SMEM)


def vmem():
    return pl.BlockSpec(memory_space=pltpu.VMEM)


def hbm():
    return pl.BlockSpec(memory_space=pl.ANY)


def pack_kernel(owner_ref, q_ref, k_ref, v_ref, out_ref, place_ref, used_ref):
    for g in range(GROUPS):
        used_ref[g] = 0
    out_ref[...] = jnp.zeros_like(out_ref)
    width = HEADS * HEAD

    @pl.loop(0, HOST, unroll=4)
    def _(c):
        prompt = owner_ref[c, 0]
        rank = used_ref[prompt]
        used_ref[prompt] = rank + 1
        place = prompt * SLOT + rank
        place_ref[c] = place
        out_ref[place, :, 0:width] = q_ref[c]
        out_ref[place, :, width : width + HEAD] = k_ref[c]
        out_ref[place, :, width + HEAD :] = v_ref[c]


def pack(owner, q, k, v):
    return pl.pallas_call(
        pack_kernel,
        out_shape=[
            jax.ShapeDtypeStruct((GROUPS * SLOT, STEPS, (HEADS + 2) * HEAD), jnp.bfloat16),
            jax.ShapeDtypeStruct((HOST,), jnp.int32),
        ],
        in_specs=[smem(), vmem(), vmem(), vmem()],
        out_specs=[vmem(), smem()],
        scratch_shapes=[pltpu.SMEM((GROUPS,), jnp.int32)],
        compiler_params=pltpu.CompilerParams(vmem_limit_bytes=16 * 2**20),
        name="pack",
    )(owner, q, k, v)


def unpack_kernel(place_ref, got_ref, out_ref):
    for c in range(HOST):
        out_ref[c] = got_ref[place_ref[c]]


def unpack(places, got):
    return pl.pallas_call(
        unpack_kernel,
        out_shape=jax.ShapeDtypeStruct((HOST,) + got.shape[1:], got.dtype),
        in_specs=[smem(), vmem()],
        out_specs=vmem(),
        compiler_params=pltpu.CompilerParams(vmem_limit_bytes=16 * 2**20),
        name="unpack",
    )(places, got)


TILE = 8
ROWS = 256
WIDE = 1024


def attend_kernel(head, heads, start, tiles, fresh, q_ref, k_ref, v_ref, *refs):
    scratch = refs[-6:]
    if fresh:
        out_ref, kt_ref, ve_ref = refs[:3]
        for first in range(0, PROMPT, 512):
            part = slice(first, first + 512)
            kt_ref[:, part] = k_ref[0, part, :].astype(jnp.float32).T.astype(jnp.bfloat16)
            ve_ref[part, 0:HEAD] = v_ref[0, part, :]
            lane = lax.broadcasted_iota(jnp.int32, (512, HEAD), 1)
            ve_ref[part, HEAD:] = jnp.where(lane == 0, 1.0, 0.0).astype(jnp.bfloat16)
    else:
        kt_ref, ve_ref, out_ref = k_ref, v_ref, refs[-7]
    if start:
        out_ref[0 : start * TILE] = refs[0][...]
    each = TILE * STEPS
    base = HEADS * HEAD
    s_refs, p_refs, peaks = scratch[0:2], scratch[2:4], scratch[4:6]

    def flat(tile, first):
        block = q_ref[pl.ds((start + tile) * TILE, TILE), :, first : first + HEAD]
        return block.astype(jnp.float32).reshape(each, HEAD)

    def weights(scores, peak):
        return jnp.exp2((scores - peak) * SCALE2).astype(jnp.bfloat16)

    def stages(tile, slot, do):
        s_ref, peak_ref = s_refs[slot], peaks[slot]
        old_s, old_peak, new_p, old_p = s_refs[1 - slot], peaks[1 - slot], p_refs[1 - slot], p_refs[slot]
        top = None
        if do[0]:
            query = jnp.concatenate(
                [flat(tile, (head + h) * HEAD) for h in range(heads)], axis=0
            ).astype(jnp.bfloat16)
            own_k = flat(tile, base)
            own_k = jnp.concatenate([own_k, jnp.zeros_like(own_k)], axis=0).astype(jnp.bfloat16)
            own = lax.dot_general(
                query, own_k, (((1,), (1,)), ((), ())), preferred_element_type=jnp.float32
            )
            row = lax.rem(lax.broadcasted_iota(jnp.int32, own.shape, 0), each)
            col = lax.broadcasted_iota(jnp.int32, own.shape, 1)
            own = jnp.where((row // STEPS == col // STEPS) & (col <= row), own, -1e30)
            s_ref[:, PROMPT:] = own
            top = own
        if do[1]:
            peak = old_peak[...]
        if do[2]:
            own_v = flat(tile - 2, base + HEAD)
            lane = lax.broadcasted_iota(jnp.int32, own_v.shape, 1)
            own_v = jnp.concatenate([own_v, jnp.where(lane == 0, 1.0, 0.0)], axis=1)
            own_v = jnp.concatenate([own_v, jnp.zeros_like(own_v)], axis=0).astype(jnp.bfloat16)
            acc = jnp.dot(old_p[:, PROMPT:], own_v, preferred_element_type=jnp.float32)
        for first in range(0, PROMPT, WIDE):
            part = slice(first, first + WIDE)
            if do[0]:
                scores = jnp.dot(query, kt_ref[:, part], preferred_element_type=jnp.float32)
                s_ref[:, part] = scores
                for lane in range(0, WIDE, HEAD):
                    top = jnp.maximum(top, scores[:, lane : lane + HEAD])
            if do[1]:
                for at in range(first, first + WIDE, HEAD):
                    new_p[:, at : at + HEAD] = weights(old_s[:, at : at + HEAD], peak)
            if do[2]:
                acc = acc + jnp.dot(
                    old_p[:, part], ve_ref[part, :], preferred_element_type=jnp.float32
                )
        if do[1]:
            new_p[:, PROMPT:] = weights(old_s[:, PROMPT:], peak)
        if do[0]:
            peak_ref[...] = jnp.broadcast_to(jnp.max(top, axis=1, keepdims=True), top.shape)
        if do[2]:
            out = acc[:, 0:HEAD] / acc[:, HEAD : HEAD + 1]
            for h in range(heads):
                out_ref[pl.ds((start + tile - 2) * TILE, TILE), :, h * HEAD : (h + 1) * HEAD] = (
                    out[h * each : (h + 1) * each].reshape(TILE, STEPS, HEAD).astype(jnp.bfloat16)
                )

    stages(0, 0, (True, False, False))
    stages(1, 1, (True, True, False))

    for pair in range(1, tiles // 2):
        stages(2 * pair, 0, (True, True, True))
        stages(2 * pair + 1, 1, (True, True, True))
    stages(tiles, 0, (False, True, True))
    stages(tiles + 1, 1, (False, False, True))


def attend(head, heads, received, keys, values, start, slots, before=(), fresh=False):
    assert heads * TILE * STEPS == ROWS
    inputs = [received, keys, values, *before]
    outs = [jax.ShapeDtypeStruct((start + slots, STEPS, heads * HEAD), jnp.bfloat16)]
    if fresh:
        outs.append(jax.ShapeDtypeStruct((HEAD, PROMPT), jnp.bfloat16))
        outs.append(jax.ShapeDtypeStruct((PROMPT, 2 * HEAD), jnp.bfloat16))
    return pl.pallas_call(
        functools.partial(attend_kernel, head, heads, start // TILE, slots // TILE, fresh),
        out_shape=outs,
        in_specs=[vmem()] * len(inputs),
        out_specs=[vmem()] * len(outs),
        scratch_shapes=[pltpu.VMEM((ROWS, PROMPT + HEAD), jnp.float32)] * 2
        + [pltpu.VMEM((ROWS, PROMPT + HEAD), jnp.bfloat16)] * 2
        + [pltpu.VMEM((ROWS, HEAD), jnp.float32)] * 2,
        compiler_params=pltpu.CompilerParams(vmem_limit_bytes=24 * 2**20),
        cost_estimate=pl.CostEstimate(
            flops=4 * slots * STEPS * heads * PROMPT * HEAD,
            bytes_accessed=4 * 2**20,
            transcendentals=slots * STEPS * heads * PROMPT,
        ),
        name="attend",
    )(*inputs)


COLS = 1024
HALF = COLS // 2


def gemm_kernel(offsets, plane_ref, a0_ref, a1_ref, weight, *refs):
    outs, (w_ref, sems) = refs[:-2], refs[-2:]
    copies = []
    for i, offset in enumerate(offsets):
        to = lax.rem(plane_ref[0] + offset, RING)
        for r in range(4):
            copy = pltpu.make_async_copy(
                weight.at[to * 4 + r], w_ref.at[i, :, pl.ds(r * 256, 256)], sems.at[i, r]
            )
            copy.start()
            copies.append(copy)
    left = jnp.concatenate([a0_ref[...], a1_ref[...]], axis=1)
    for i, _ in enumerate(offsets):
        for part in range(2):
            for copy in copies[i * 4 + part * 2 : i * 4 + part * 2 + 2]:
                copy.wait()
            cols = slice(part * HALF, (part + 1) * HALF)
            share = jnp.dot(left, w_ref[i, :, cols], preferred_element_type=jnp.float32)
            if len(outs) == 4:
                middle = share.shape[0] // 2
                outs[part][...] = share[:middle].astype(jnp.bfloat16)
                outs[2 + part][...] = share[middle:].astype(jnp.bfloat16)
            else:
                outs[i][:, cols] = share


def gemm(offsets, plane, home, weight):
    rows = home[0].shape[0]
    if offsets == (RING // 2,):
        outs = [jax.ShapeDtypeStruct((rows // 2, HALF), jnp.bfloat16)] * 4
    else:
        outs = [jax.ShapeDtypeStruct((rows, COLS), jnp.float32)] * len(offsets)
    depth = weight.shape[1]
    return pl.pallas_call(
        functools.partial(gemm_kernel, offsets),
        out_shape=outs,
        in_specs=[smem(), vmem(), vmem(), hbm()],
        out_specs=[vmem()] * len(outs),
        scratch_shapes=[
            pltpu.VMEM((len(offsets), depth, COLS), jnp.bfloat16),
            pltpu.SemaphoreType.DMA((len(offsets), 4)),
        ],
        compiler_params=pltpu.CompilerParams(vmem_limit_bytes=48 * 2**20),
        cost_estimate=pl.CostEstimate(
            flops=2 * rows * COLS * depth * len(offsets),
            bytes_accessed=depth * COLS * 2 * len(offsets),
            transcendentals=0,
        ),
        name="gemm",
    )(plane, *home, weight)


def join_kernel(part, up_ref, down_ref, got_up_ref, got_down_ref, out_up_ref, out_down_ref):
    cols = slice(part * HALF, (part + 1) * HALF)
    rows = got_up_ref.shape[0]
    whole = up_ref.shape[0]
    out_up_ref[0:rows, :] = (up_ref[0:rows, cols] + got_up_ref[...].astype(jnp.float32)).astype(jnp.bfloat16)
    out_down_ref[whole - rows :, :] = (
        down_ref[whole - rows :, cols] + got_down_ref[...].astype(jnp.float32)
    ).astype(jnp.bfloat16)
    if rows < whole:
        out_up_ref[rows:, :] = up_ref[rows:, cols].astype(jnp.bfloat16)
        out_down_ref[0 : whole - rows, :] = down_ref[0 : whole - rows, cols].astype(jnp.bfloat16)


def join(part, shares, got):
    out = jax.ShapeDtypeStruct((shares[0].shape[0], HALF), jnp.bfloat16)
    return pl.pallas_call(
        functools.partial(join_kernel, part),
        out_shape=[out, out],
        in_specs=[vmem()] * 4,
        out_specs=[vmem()] * 2,
        compiler_params=pltpu.CompilerParams(vmem_limit_bytes=8 * 2**20),
        name="join",
    )(*shares, *got)


def finish_kernel(share_ref, *refs):
    got, out_ref = refs[:-1], refs[-1]
    for part in range(2):
        cols = slice(part * HALF, (part + 1) * HALF)
        total = share_ref[:, cols]
        for ref in got[2 * part : 2 * part + 2]:
            total = total + ref[...].astype(jnp.float32)
        out_ref[:, cols] = total.astype(jnp.bfloat16)


def finish(share, got):
    return pl.pallas_call(
        finish_kernel,
        out_shape=jax.ShapeDtypeStruct(share.shape, jnp.bfloat16),
        in_specs=[vmem()] * (1 + len(got)),
        out_specs=vmem(),
        compiler_params=pltpu.CompilerParams(vmem_limit_bytes=8 * 2**20),
        name="finish",
    )(share, *got)


def hop(up, down):
    ahead = [(i, (i + 1) % RING) for i in range(RING)]
    back = [((i + 1) % RING, i) for i in range(RING)]
    return lax.ppermute(up, "z", ahead), lax.ppermute(down, "z", back)


def exchange(block):
    shape = block.shape
    sent = block.reshape((GROUPS, SLOT) + shape[1:])
    got = lax.all_to_all(sent, GROUP, split_axis=0, concat_axis=0, tiled=True)
    return got.reshape(shape)


def shards(owner, cont_q, own_keys, own_values, prompt_keys, prompt_values, out_weight):
    tie = lax.optimization_barrier
    slots = GROUPS * SLOT
    rows = HOST * STEPS
    plane = lax.axis_index("z").astype(jnp.int32).reshape(1)
    weight = lax.all_gather(out_weight, GROUP, axis=0)
    packed, places = pack(owner, cont_q, own_keys, own_values)
    received = exchange(packed)

    attn, keys, values = attend(
        0, PARTS[0], received, prompt_keys, prompt_values, 0, slots, fresh=True
    )
    back = exchange(attn)
    (attn,) = attend(PARTS[0], PARTS[1], received, keys, values, 0, slots)
    back, _ = tie((back, attn))
    home = [unpack(places, back).reshape(rows, PARTS[0] * HEAD)]
    home.append(unpack(places, exchange(attn)).reshape(rows, PARTS[1] * HEAD))

    quarters = gemm((RING // 2,), plane, home, weight)
    got = [hop(quarters[part], quarters[2 + part]) for part in range(2)]
    for away in (3, 2, 1):
        shares = gemm((away, RING - away), plane, home, weight)
        got = [hop(*join(part, shares, got[part])) for part in range(2)]
    (share,) = gemm((0,), plane, home, weight)
    return finish(share, [*got[0], *got[1]])


def solution(mesh):
    mesh = Mesh(mesh.devices.reshape(4, 4, 2, 8), ("y", "x", "c", "z"))
    in_specs = (
        P(GROUP, None),
        P(GROUP, None, "z"),
        P(GROUP, None, "z"),
        P(GROUP, None, "z"),
        P(GROUP, None, "z"),
        P(GROUP, None, "z"),
        P("z", GROUP),
    )
    return jax.shard_map(
        shards, mesh=mesh, in_specs=in_specs, out_specs=P(GROUP, "z"), check_vma=False
    )
```

```python
import functools

import jax
import jax.numpy as jnp
from jax import lax
from jax.experimental import pallas as pl
from jax.experimental.pallas import tpu as pltpu
from jax.sharding import Mesh, PartitionSpec as P

HEAD = 128
GROUPS = 32
SLOT = 2
HOST = 32
STEPS = 8
HEADS = 8
PROMPT = 4096
RING = 8
GROUP = ("y", "x", "c")
PARTS = (4, 4)
SCALE2 = HEAD**-0.5 * 1.4426950408889634


def smem():
    return pl.BlockSpec(memory_space=pltpu.SMEM)


def vmem():
    return pl.BlockSpec(memory_space=pltpu.VMEM)


def hbm():
    return pl.BlockSpec(memory_space=pl.ANY)


def pack_kernel(owner_ref, q_ref, k_ref, v_ref, out_ref, place_ref, used_ref):
    for g in range(GROUPS):
        used_ref[g] = 0
    out_ref[...] = jnp.zeros_like(out_ref)
    width = HEADS * HEAD

    @pl.loop(0, HOST, unroll=4)
    def _(c):
        prompt = owner_ref[c, 0]
        rank = used_ref[prompt]
        used_ref[prompt] = rank + 1
        place = prompt * SLOT + rank
        place_ref[c] = place
        out_ref[place, :, 0:width] = q_ref[c]
        out_ref[place, :, width : width + HEAD] = k_ref[c]
        out_ref[place, :, width + HEAD :] = v_ref[c]


def pack(owner, q, k, v):
    return pl.pallas_call(
        pack_kernel,
        out_shape=[
            jax.ShapeDtypeStruct((GROUPS * SLOT, STEPS, (HEADS + 2) * HEAD), jnp.bfloat16),
            jax.ShapeDtypeStruct((HOST,), jnp.int32),
        ],
        in_specs=[smem(), vmem(), vmem(), vmem()],
        out_specs=[vmem(), smem()],
        scratch_shapes=[pltpu.SMEM((GROUPS,), jnp.int32)],
        compiler_params=pltpu.CompilerParams(vmem_limit_bytes=16 * 2**20),
        name="pack",
    )(owner, q, k, v)


def unpack_kernel(place_ref, got_ref, out_ref):
    for c in range(HOST):
        out_ref[c] = got_ref[place_ref[c]]


def unpack(places, got):
    return pl.pallas_call(
        unpack_kernel,
        out_shape=jax.ShapeDtypeStruct((HOST,) + got.shape[1:], got.dtype),
        in_specs=[smem(), vmem()],
        out_specs=vmem(),
        compiler_params=pltpu.CompilerParams(vmem_limit_bytes=16 * 2**20),
        name="unpack",
    )(places, got)


TILE = 8
ROWS = 256
WIDE = 1024


def attend_kernel(head, heads, start, tiles, fresh, q_ref, k_ref, v_ref, *refs):
    scratch = refs[-6:]
    if fresh:
        out_ref, kt_ref, ve_ref = refs[:3]
        for first in range(0, PROMPT, 512):
            part = slice(first, first + 512)
            kt_ref[:, part] = k_ref[0, part, :].astype(jnp.float32).T.astype(jnp.bfloat16)
            ve_ref[part, 0:HEAD] = v_ref[0, part, :]
            lane = lax.broadcasted_iota(jnp.int32, (512, HEAD), 1)
            ve_ref[part, HEAD:] = jnp.where(lane == 0, 1.0, 0.0).astype(jnp.bfloat16)
    else:
        kt_ref, ve_ref, out_ref = k_ref, v_ref, refs[-7]
    if start:
        out_ref[0 : start * TILE] = refs[0][...]
    each = TILE * STEPS
    base = HEADS * HEAD
    s_refs, p_refs, peaks = scratch[0:2], scratch[2:4], scratch[4:6]

    def flat(tile, first):
        block = q_ref[pl.ds((start + tile) * TILE, TILE), :, first : first + HEAD]
        return block.astype(jnp.float32).reshape(each, HEAD)

    def weights(scores, peak):
        return jnp.exp2((scores - peak) * SCALE2).astype(jnp.bfloat16)

    def stages(tile, slot, do):
        s_ref, peak_ref = s_refs[slot], peaks[slot]
        old_s, old_peak, new_p, old_p = s_refs[1 - slot], peaks[1 - slot], p_refs[1 - slot], p_refs[slot]
        top = None
        if do[0]:
            query = jnp.concatenate(
                [flat(tile, (head + h) * HEAD) for h in range(heads)], axis=0
            ).astype(jnp.bfloat16)
            own_k = flat(tile, base)
            own_k = jnp.concatenate([own_k, jnp.zeros_like(own_k)], axis=0).astype(jnp.bfloat16)
            own = lax.dot_general(
                query, own_k, (((1,), (1,)), ((), ())), preferred_element_type=jnp.float32
            )
            row = lax.rem(lax.broadcasted_iota(jnp.int32, own.shape, 0), each)
            col = lax.broadcasted_iota(jnp.int32, own.shape, 1)
            own = jnp.where((row // STEPS == col // STEPS) & (col <= row), own, -1e30)
            s_ref[:, PROMPT:] = own
            top = own
        if do[1]:
            peak = old_peak[...]
        if do[2]:
            own_v = flat(tile - 2, base + HEAD)
            lane = lax.broadcasted_iota(jnp.int32, own_v.shape, 1)
            own_v = jnp.concatenate([own_v, jnp.where(lane == 0, 1.0, 0.0)], axis=1)
            own_v = jnp.concatenate([own_v, jnp.zeros_like(own_v)], axis=0).astype(jnp.bfloat16)
            acc = jnp.dot(old_p[:, PROMPT:], own_v, preferred_element_type=jnp.float32)
        for first in range(0, PROMPT, WIDE):
            part = slice(first, first + WIDE)
            if do[0]:
                scores = jnp.dot(query, kt_ref[:, part], preferred_element_type=jnp.float32)
                s_ref[:, part] = scores
                for lane in range(0, WIDE, HEAD):
                    top = jnp.maximum(top, scores[:, lane : lane + HEAD])
            if do[1]:
                for at in range(first, first + WIDE, HEAD):
                    new_p[:, at : at + HEAD] = weights(old_s[:, at : at + HEAD], peak)
            if do[2]:
                acc = acc + jnp.dot(
                    old_p[:, part], ve_ref[part, :], preferred_element_type=jnp.float32
                )
        if do[1]:
            new_p[:, PROMPT:] = weights(old_s[:, PROMPT:], peak)
        if do[0]:
            peak_ref[...] = jnp.broadcast_to(jnp.max(top, axis=1, keepdims=True), top.shape)
        if do[2]:
            out = acc[:, 0:HEAD] / acc[:, HEAD : HEAD + 1]
            for h in range(heads):
                out_ref[pl.ds((start + tile - 2) * TILE, TILE), :, h * HEAD : (h + 1) * HEAD] = (
                    out[h * each : (h + 1) * each].reshape(TILE, STEPS, HEAD).astype(jnp.bfloat16)
                )

    stages(0, 0, (True, False, False))
    stages(1, 1, (True, True, False))

    for pair in range(1, tiles // 2):
        stages(2 * pair, 0, (True, True, True))
        stages(2 * pair + 1, 1, (True, True, True))
    stages(tiles, 0, (False, True, True))
    stages(tiles + 1, 1, (False, False, True))


def attend(head, heads, received, keys, values, start, slots, before=(), fresh=False):
    assert heads * TILE * STEPS == ROWS
    inputs = [received, keys, values, *before]
    outs = [jax.ShapeDtypeStruct((start + slots, STEPS, heads * HEAD), jnp.bfloat16)]
    if fresh:
        outs.append(jax.ShapeDtypeStruct((HEAD, PROMPT), jnp.bfloat16))
        outs.append(jax.ShapeDtypeStruct((PROMPT, 2 * HEAD), jnp.bfloat16))
    return pl.pallas_call(
        functools.partial(attend_kernel, head, heads, start // TILE, slots // TILE, fresh),
        out_shape=outs,
        in_specs=[vmem()] * len(inputs),
        out_specs=[vmem()] * len(outs),
        scratch_shapes=[pltpu.VMEM((ROWS, PROMPT + HEAD), jnp.float32)] * 2
        + [pltpu.VMEM((ROWS, PROMPT + HEAD), jnp.bfloat16)] * 2
        + [pltpu.VMEM((ROWS, HEAD), jnp.float32)] * 2,
        compiler_params=pltpu.CompilerParams(vmem_limit_bytes=24 * 2**20),
        cost_estimate=pl.CostEstimate(
            flops=4 * slots * STEPS * heads * PROMPT * HEAD,
            bytes_accessed=4 * 2**20,
            transcendentals=slots * STEPS * heads * PROMPT,
        ),
        name="attend",
    )(*inputs)


COLS = 512
HALF = COLS // 2


def gemm_kernel(offsets, plane_ref, a0_ref, a1_ref, b0_ref, b1_ref, weight, *refs):
    outs, (w_ref, sems) = refs[:-2], refs[-2:]
    copies = {}
    for i, offset in enumerate(offsets):
        to = lax.rem(plane_ref[0] + offset, RING)
        for part in range(2):
            copies[i, part] = pltpu.make_async_copy(
                weight.at[to * 2 + part], w_ref.at[i, part], sems.at[i, part]
            )
            copies[i, part].start()
    left = jnp.concatenate(
        [
            jnp.concatenate([a0_ref[...], a1_ref[...]], axis=1),
            jnp.concatenate([b0_ref[...], b1_ref[...]], axis=1),
        ],
        axis=0,
    )
    for i, _ in enumerate(offsets):
        for part in range(2):
            copies[i, part].wait()
            cols = slice(part * HALF, (part + 1) * HALF)
            share = jnp.dot(left, w_ref[i, part], preferred_element_type=jnp.float32)
            if len(outs) == 4:
                middle = share.shape[0] // 2
                outs[part][...] = share[:middle].astype(jnp.bfloat16)
                outs[2 + part][...] = share[middle:].astype(jnp.bfloat16)
            else:
                outs[i][:, cols] = share


def gemm(offsets, plane, home, weight):
    rows = 2 * home[0].shape[0]
    if offsets == (RING // 2,):
        outs = [jax.ShapeDtypeStruct((rows // 2, HALF), jnp.bfloat16)] * 4
    else:
        outs = [jax.ShapeDtypeStruct((rows, COLS), jnp.float32)] * len(offsets)
    depth = weight.shape[1]
    return pl.pallas_call(
        functools.partial(gemm_kernel, offsets),
        out_shape=outs,
        in_specs=[smem()] + [vmem()] * 4 + [hbm()],
        out_specs=[vmem()] * len(outs),
        scratch_shapes=[
            pltpu.VMEM((len(offsets), 2, depth, HALF), jnp.bfloat16),
            pltpu.SemaphoreType.DMA((len(offsets), 2)),
        ],
        compiler_params=pltpu.CompilerParams(vmem_limit_bytes=48 * 2**20),
        cost_estimate=pl.CostEstimate(
            flops=2 * rows * COLS * depth * len(offsets),
            bytes_accessed=depth * COLS * 2 * len(offsets),
            transcendentals=0,
        ),
        name="gemm",
    )(plane, *home, weight)


def join_kernel(part, up_ref, down_ref, got_up_ref, got_down_ref, out_up_ref, out_down_ref):
    cols = slice(part * HALF, (part + 1) * HALF)
    rows = got_up_ref.shape[0]
    whole = up_ref.shape[0]
    out_up_ref[0:rows, :] = (up_ref[0:rows, cols] + got_up_ref[...].astype(jnp.float32)).astype(jnp.bfloat16)
    out_down_ref[whole - rows :, :] = (
        down_ref[whole - rows :, cols] + got_down_ref[...].astype(jnp.float32)
    ).astype(jnp.bfloat16)
    if rows < whole:
        out_up_ref[rows:, :] = up_ref[rows:, cols].astype(jnp.bfloat16)
        out_down_ref[0 : whole - rows, :] = down_ref[0 : whole - rows, cols].astype(jnp.bfloat16)


def join(part, shares, got):
    out = jax.ShapeDtypeStruct((shares[0].shape[0], HALF), jnp.bfloat16)
    return pl.pallas_call(
        functools.partial(join_kernel, part),
        out_shape=[out, out],
        in_specs=[vmem()] * 4,
        out_specs=[vmem()] * 2,
        compiler_params=pltpu.CompilerParams(vmem_limit_bytes=8 * 2**20),
        name="join",
    )(*shares, *got)


def finish_kernel(share_ref, *refs):
    got, (keep_ref, send_ref) = refs[:-2], refs[-2:]
    rows = keep_ref.shape[0]
    for part in range(2):
        cols = slice(part * HALF, (part + 1) * HALF)
        total = share_ref[:, cols]
        for ref in got[2 * part : 2 * part + 2]:
            total = total + ref[...].astype(jnp.float32)
        total = total.astype(jnp.bfloat16)
        keep_ref[:, cols] = total[:rows]
        send_ref[:, cols] = total[rows:]


def finish(share, got):
    out = jax.ShapeDtypeStruct((share.shape[0] // 2, COLS), jnp.bfloat16)
    return pl.pallas_call(
        finish_kernel,
        out_shape=[out, out],
        in_specs=[vmem()] * (1 + len(got)),
        out_specs=[vmem()] * 2,
        compiler_params=pltpu.CompilerParams(vmem_limit_bytes=8 * 2**20),
        name="finish",
    )(share, *got)


def lay_kernel(core_ref, mine_ref, other_ref, out_ref):
    for ref, core in ((mine_ref, core_ref[0]), (other_ref, 1 - core_ref[0])):
        for part in range(2):
            at = pl.multiple_of((part * 2 + core) * HALF, HALF)
            out_ref[:, pl.ds(at, HALF)] = ref[:, part * HALF : (part + 1) * HALF]


def lay(core, mine, other):
    return pl.pallas_call(
        lay_kernel,
        out_shape=jax.ShapeDtypeStruct((mine.shape[0], 2 * COLS), jnp.bfloat16),
        in_specs=[smem(), vmem(), vmem()],
        out_specs=vmem(),
        compiler_params=pltpu.CompilerParams(vmem_limit_bytes=8 * 2**20),
        name="lay",
    )(core, mine, other)


def swap(block):
    return lax.ppermute(block, "c", [(0, 1), (1, 0)])


def hop(up, down):
    ahead = [(i, (i + 1) % RING) for i in range(RING)]
    back = [((i + 1) % RING, i) for i in range(RING)]
    return lax.ppermute(up, "z", ahead), lax.ppermute(down, "z", back)


def exchange(block):
    shape = block.shape
    sent = block.reshape((GROUPS, SLOT) + shape[1:])
    got = lax.all_to_all(sent, GROUP, split_axis=0, concat_axis=0, tiled=True)
    return got.reshape(shape)


def shards(owner, cont_q, own_keys, own_values, prompt_keys, prompt_values, out_weight):
    tie = lax.optimization_barrier
    slots = GROUPS * SLOT
    rows = HOST * STEPS
    plane = lax.axis_index("z").astype(jnp.int32).reshape(1)
    core = lax.axis_index("c").astype(jnp.int32).reshape(1)
    weight = lax.all_gather(out_weight, ("y", "x"), axis=0)
    packed, places = pack(owner, cont_q, own_keys, own_values)
    received = exchange(packed)

    attn, keys, values = attend(
        0, PARTS[0], received, prompt_keys, prompt_values, 0, slots, fresh=True
    )
    back = exchange(attn)
    (attn,) = attend(PARTS[0], PARTS[1], received, keys, values, 0, slots)
    back, _ = tie((back, attn))
    home = [unpack(places, back).reshape(rows, PARTS[0] * HEAD)]
    home.append(unpack(places, exchange(attn)).reshape(rows, PARTS[1] * HEAD))
    home += [swap(home[0]), swap(home[1])]

    quarters = gemm((RING // 2,), plane, home, weight)
    got = [hop(quarters[part], quarters[2 + part]) for part in range(2)]
    for away in (3, 2, 1):
        shares = gemm((away, RING - away), plane, home, weight)
        got = [hop(*join(part, shares, got[part])) for part in range(2)]
    (share,) = gemm((0,), plane, home, weight)
    keep, send = finish(share, [*got[0], *got[1]])
    return lay(core, keep, swap(send))


def solution(mesh):
    mesh = Mesh(mesh.devices.reshape(4, 4, 2, 8), ("y", "x", "c", "z"))
    in_specs = (
        P(GROUP, None),
        P(GROUP, None, "z"),
        P(GROUP, None, "z"),
        P(GROUP, None, "z"),
        P(GROUP, None, "z"),
        P(GROUP, None, "z"),
        P("z", GROUP),
    )
    return jax.shard_map(
        shards, mesh=mesh, in_specs=in_specs, out_specs=P(GROUP, "z"), check_vma=False
    )
```

```python
import functools

import jax
import jax.numpy as jnp
from jax import lax
from jax.experimental import pallas as pl
from jax.experimental.pallas import tpu as pltpu
from jax.sharding import Mesh, PartitionSpec as P

HEAD = 128
GROUPS = 32
SLOT = 2
HOST = 32
STEPS = 8
HEADS = 8
PROMPT = 4096
RING = 8
GROUP = ("y", "x", "c")
PARTS = (4, 4)
SCALE2 = HEAD**-0.5 * 1.4426950408889634


def smem():
    return pl.BlockSpec(memory_space=pltpu.SMEM)


def vmem():
    return pl.BlockSpec(memory_space=pltpu.VMEM)


def hbm():
    return pl.BlockSpec(memory_space=pl.ANY)


def pack_kernel(owner_ref, q_ref, k_ref, v_ref, out_ref, place_ref, used_ref):
    for g in range(GROUPS):
        used_ref[g] = 0
    out_ref[...] = jnp.zeros_like(out_ref)
    width = HEADS * HEAD

    @pl.loop(0, HOST, unroll=4)
    def _(c):
        prompt = owner_ref[c, 0]
        rank = used_ref[prompt]
        used_ref[prompt] = rank + 1
        place = prompt * SLOT + rank
        place_ref[c] = place
        out_ref[place, :, 0:width] = q_ref[c]
        out_ref[place, :, width : width + HEAD] = k_ref[c]
        out_ref[place, :, width + HEAD :] = v_ref[c]


def pack(owner, q, k, v):
    return pl.pallas_call(
        pack_kernel,
        out_shape=[
            jax.ShapeDtypeStruct((GROUPS * SLOT, STEPS, (HEADS + 2) * HEAD), jnp.bfloat16),
            jax.ShapeDtypeStruct((HOST,), jnp.int32),
        ],
        in_specs=[smem(), vmem(), vmem(), vmem()],
        out_specs=[vmem(), smem()],
        scratch_shapes=[pltpu.SMEM((GROUPS,), jnp.int32)],
        compiler_params=pltpu.CompilerParams(vmem_limit_bytes=16 * 2**20),
        name="pack",
    )(owner, q, k, v)


def unpack_kernel(place_ref, got_ref, out_ref):
    for c in range(HOST):
        out_ref[c] = got_ref[place_ref[c]]


def unpack(places, got):
    return pl.pallas_call(
        unpack_kernel,
        out_shape=jax.ShapeDtypeStruct((HOST,) + got.shape[1:], got.dtype),
        in_specs=[smem(), vmem()],
        out_specs=vmem(),
        compiler_params=pltpu.CompilerParams(vmem_limit_bytes=16 * 2**20),
        name="unpack",
    )(places, got)


TILE = 8
ROWS = 256
WIDE = 1024


def attend_kernel(head, heads, start, tiles, fresh, q_ref, k_ref, v_ref, *refs):
    scratch = refs[-6:]
    if fresh:
        out_ref, kt_ref, ve_ref = refs[:3]
        for first in range(0, PROMPT, 512):
            part = slice(first, first + 512)
            kt_ref[:, part] = k_ref[0, part, :].astype(jnp.float32).T.astype(jnp.bfloat16)
            ve_ref[part, 0:HEAD] = v_ref[0, part, :]
            lane = lax.broadcasted_iota(jnp.int32, (512, HEAD), 1)
            ve_ref[part, HEAD:] = jnp.where(lane == 0, 1.0, 0.0).astype(jnp.bfloat16)
    else:
        kt_ref, ve_ref, out_ref = k_ref, v_ref, refs[-7]
    if start:
        out_ref[0 : start * TILE] = refs[0][...]
    each = TILE * STEPS
    base = HEADS * HEAD
    s_refs, p_refs, peaks = scratch[0:2], scratch[2:4], scratch[4:6]

    def flat(tile, first):
        block = q_ref[pl.ds((start + tile) * TILE, TILE), :, first : first + HEAD]
        return block.astype(jnp.float32).reshape(each, HEAD)

    def weights(scores, peak):
        return jnp.exp2((scores - peak) * SCALE2).astype(jnp.bfloat16)

    def stages(tile, slot, do):
        s_ref, peak_ref = s_refs[slot], peaks[slot]
        old_s, old_peak, new_p, old_p = s_refs[1 - slot], peaks[1 - slot], p_refs[1 - slot], p_refs[slot]
        top = None
        if do[0]:
            query = jnp.concatenate(
                [flat(tile, (head + h) * HEAD) for h in range(heads)], axis=0
            ).astype(jnp.bfloat16)
            own_k = flat(tile, base)
            own_k = jnp.concatenate([own_k, jnp.zeros_like(own_k)], axis=0).astype(jnp.bfloat16)
            own = lax.dot_general(
                query, own_k, (((1,), (1,)), ((), ())), preferred_element_type=jnp.float32
            )
            row = lax.rem(lax.broadcasted_iota(jnp.int32, own.shape, 0), each)
            col = lax.broadcasted_iota(jnp.int32, own.shape, 1)
            own = jnp.where((row // STEPS == col // STEPS) & (col <= row), own, -1e30)
            s_ref[:, PROMPT:] = own
            top = own
        if do[1]:
            peak = old_peak[...]
        if do[2]:
            own_v = flat(tile - 2, base + HEAD)
            lane = lax.broadcasted_iota(jnp.int32, own_v.shape, 1)
            own_v = jnp.concatenate([own_v, jnp.where(lane == 0, 1.0, 0.0)], axis=1)
            own_v = jnp.concatenate([own_v, jnp.zeros_like(own_v)], axis=0).astype(jnp.bfloat16)
            acc = jnp.dot(old_p[:, PROMPT:], own_v, preferred_element_type=jnp.float32)
        for first in range(0, PROMPT, WIDE):
            part = slice(first, first + WIDE)
            if do[0]:
                scores = jnp.dot(query, kt_ref[:, part], preferred_element_type=jnp.float32)
                s_ref[:, part] = scores
                for lane in range(0, WIDE, HEAD):
                    top = jnp.maximum(top, scores[:, lane : lane + HEAD])
            if do[1]:
                for at in range(first, first + WIDE, HEAD):
                    new_p[:, at : at + HEAD] = weights(old_s[:, at : at + HEAD], peak)
            if do[2]:
                acc = acc + jnp.dot(
                    old_p[:, part], ve_ref[part, :], preferred_element_type=jnp.float32
                )
        if do[1]:
            new_p[:, PROMPT:] = weights(old_s[:, PROMPT:], peak)
        if do[0]:
            peak_ref[...] = jnp.broadcast_to(jnp.max(top, axis=1, keepdims=True), top.shape)
        if do[2]:
            out = acc[:, 0:HEAD] / acc[:, HEAD : HEAD + 1]
            for h in range(heads):
                out_ref[pl.ds((start + tile - 2) * TILE, TILE), :, h * HEAD : (h + 1) * HEAD] = (
                    out[h * each : (h + 1) * each].reshape(TILE, STEPS, HEAD).astype(jnp.bfloat16)
                )

    stages(0, 0, (True, False, False))
    stages(1, 1, (True, True, False))

    for pair in range(1, tiles // 2):
        stages(2 * pair, 0, (True, True, True))
        stages(2 * pair + 1, 1, (True, True, True))
    stages(tiles, 0, (False, True, True))
    stages(tiles + 1, 1, (False, False, True))


def attend(head, heads, received, keys, values, start, slots, before=(), fresh=False):
    assert heads * TILE * STEPS == ROWS
    inputs = [received, keys, values, *before]
    outs = [jax.ShapeDtypeStruct((start + slots, STEPS, heads * HEAD), jnp.bfloat16)]
    if fresh:
        outs.append(jax.ShapeDtypeStruct((HEAD, PROMPT), jnp.bfloat16))
        outs.append(jax.ShapeDtypeStruct((PROMPT, 2 * HEAD), jnp.bfloat16))
    return pl.pallas_call(
        functools.partial(attend_kernel, head, heads, start // TILE, slots // TILE, fresh),
        out_shape=outs,
        in_specs=[vmem()] * len(inputs),
        out_specs=[vmem()] * len(outs),
        scratch_shapes=[pltpu.VMEM((ROWS, PROMPT + HEAD), jnp.float32)] * 2
        + [pltpu.VMEM((ROWS, PROMPT + HEAD), jnp.bfloat16)] * 2
        + [pltpu.VMEM((ROWS, HEAD), jnp.float32)] * 2,
        compiler_params=pltpu.CompilerParams(vmem_limit_bytes=24 * 2**20),
        cost_estimate=pl.CostEstimate(
            flops=4 * slots * STEPS * heads * PROMPT * HEAD,
            bytes_accessed=4 * 2**20,
            transcendentals=slots * STEPS * heads * PROMPT,
        ),
        name="attend",
    )(*inputs)


COLS = 1024
HALF = COLS // 2


def gemm_kernel(offsets, parts, plane_ref, a0_ref, a1_ref, weight, *refs):
    outs, (w_ref, sems) = refs[:-2], refs[-2:]
    copies = {}
    for i, offset in enumerate(offsets):
        to = lax.rem(plane_ref[0] + offset, RING)
        for j, part in enumerate(parts):
            for r in range(2):
                copies[i, j, r] = pltpu.make_async_copy(
                    weight.at[to * 4 + part * 2 + r],
                    w_ref.at[i, j, :, pl.ds(r * 256, 256)],
                    sems.at[i, j, r],
                )
                copies[i, j, r].start()
    left = jnp.concatenate([a0_ref[...], a1_ref[...]], axis=1)
    for i, _ in enumerate(offsets):
        for j, _ in enumerate(parts):
            for r in range(2):
                copies[i, j, r].wait()
            share = jnp.dot(left, w_ref[i, j], preferred_element_type=jnp.float32)
            if offsets == (RING // 2,):
                middle = share.shape[0] // 2
                outs[0][...] = share[:middle].astype(jnp.bfloat16)
                outs[1][...] = share[middle:].astype(jnp.bfloat16)
            else:
                outs[i][:, j * HALF : (j + 1) * HALF] = share


def gemm(offsets, parts, plane, home, weight):
    rows = home[0].shape[0]
    if offsets == (RING // 2,):
        outs = [jax.ShapeDtypeStruct((rows // 2, HALF), jnp.bfloat16)] * 2
    else:
        outs = [jax.ShapeDtypeStruct((rows, HALF * len(parts)), jnp.float32)] * len(offsets)
    depth = weight.shape[1]
    return pl.pallas_call(
        functools.partial(gemm_kernel, offsets, parts),
        out_shape=outs,
        in_specs=[smem(), vmem(), vmem(), hbm()],
        out_specs=[vmem()] * len(outs),
        scratch_shapes=[
            pltpu.VMEM((len(offsets), len(parts), depth, HALF), jnp.bfloat16),
            pltpu.SemaphoreType.DMA((len(offsets), len(parts), 2)),
        ],
        compiler_params=pltpu.CompilerParams(vmem_limit_bytes=48 * 2**20),
        cost_estimate=pl.CostEstimate(
            flops=2 * rows * HALF * len(parts) * depth * len(offsets),
            bytes_accessed=depth * HALF * len(parts) * 2 * len(offsets),
            transcendentals=0,
        ),
        name="gemm",
    )(plane, *home, weight)


def join_kernel(up_ref, down_ref, got_up_ref, got_down_ref, out_up_ref, out_down_ref):
    rows = got_up_ref.shape[0]
    whole = up_ref.shape[0]
    out_up_ref[0:rows, :] = (up_ref[0:rows, :] + got_up_ref[...].astype(jnp.float32)).astype(jnp.bfloat16)
    out_down_ref[whole - rows :, :] = (
        down_ref[whole - rows :, :] + got_down_ref[...].astype(jnp.float32)
    ).astype(jnp.bfloat16)
    if rows < whole:
        out_up_ref[rows:, :] = up_ref[rows:, :].astype(jnp.bfloat16)
        out_down_ref[0 : whole - rows, :] = down_ref[0 : whole - rows, :].astype(jnp.bfloat16)


def join(shares, got):
    out = jax.ShapeDtypeStruct(shares[0].shape, jnp.bfloat16)
    return pl.pallas_call(
        join_kernel,
        out_shape=[out, out],
        in_specs=[vmem()] * 4,
        out_specs=[vmem()] * 2,
        compiler_params=pltpu.CompilerParams(vmem_limit_bytes=8 * 2**20),
        name="join",
    )(*shares, *got)


def finish_kernel(share_ref, *refs):
    got, out_ref = refs[:-1], refs[-1]
    for part in range(2):
        cols = slice(part * HALF, (part + 1) * HALF)
        total = share_ref[:, cols]
        for ref in got[2 * part : 2 * part + 2]:
            total = total + ref[...].astype(jnp.float32)
        out_ref[:, cols] = total.astype(jnp.bfloat16)


def finish(share, got):
    return pl.pallas_call(
        finish_kernel,
        out_shape=jax.ShapeDtypeStruct(share.shape, jnp.bfloat16),
        in_specs=[vmem()] * (1 + len(got)),
        out_specs=vmem(),
        compiler_params=pltpu.CompilerParams(vmem_limit_bytes=8 * 2**20),
        name="finish",
    )(share, *got)


def hop(up, down):
    ahead = [(i, (i + 1) % RING) for i in range(RING)]
    back = [((i + 1) % RING, i) for i in range(RING)]
    return lax.ppermute(up, "z", ahead), lax.ppermute(down, "z", back)


def exchange(block):
    shape = block.shape
    sent = block.reshape((GROUPS, SLOT) + shape[1:])
    got = lax.all_to_all(sent, GROUP, split_axis=0, concat_axis=0, tiled=True)
    return got.reshape(shape)


def shards(owner, cont_q, own_keys, own_values, prompt_keys, prompt_values, out_weight):
    tie = lax.optimization_barrier
    slots = GROUPS * SLOT
    rows = HOST * STEPS
    plane = lax.axis_index("z").astype(jnp.int32).reshape(1)
    weight = lax.all_gather(out_weight, GROUP, axis=0)
    packed, places = pack(owner, cont_q, own_keys, own_values)
    received = exchange(packed)

    attn, keys, values = attend(
        0, PARTS[0], received, prompt_keys, prompt_values, 0, slots, fresh=True
    )
    back = exchange(attn)
    (attn,) = attend(PARTS[0], PARTS[1], received, keys, values, 0, slots)
    back, _ = tie((back, attn))
    home = [unpack(places, back).reshape(rows, PARTS[0] * HEAD)]
    home.append(unpack(places, exchange(attn)).reshape(rows, PARTS[1] * HEAD))

    got = [hop(*gemm((RING // 2,), (part,), plane, home, weight)) for part in range(2)]
    for away in (3, 2, 1):
        offsets = (away, RING - away)
        sums = join(gemm(offsets, (0,), plane, home, weight), got[0])
        *home, up, down = tie((*home, *sums))
        sums = join(gemm(offsets, (1,), plane, home, weight), got[1])
        got = [hop(up, down), hop(*sums)]
    (share,) = gemm((0,), (0, 1), plane, home, weight)
    return finish(share, [*got[0], *got[1]])


def solution(mesh):
    mesh = Mesh(mesh.devices.reshape(4, 4, 2, 8), ("y", "x", "c", "z"))
    in_specs = (
        P(GROUP, None),
        P(GROUP, None, "z"),
        P(GROUP, None, "z"),
        P(GROUP, None, "z"),
        P(GROUP, None, "z"),
        P(GROUP, None, "z"),
        P("z", GROUP),
    )
    return jax.shard_map(
        shards, mesh=mesh, in_specs=in_specs, out_specs=P(GROUP, "z"), check_vma=False
    )
```
